512 devices in a mesh: section: 32 (over x, y, core), tensor: 16 (over z).
Axes of the slice: x: 4, y: 4, z: 16, core: 2. Of those that a mesh axis runs over, the one named last changes fastest.
Arguments:
- section_inputs: bfloat16 [32, 1, 512, 2304], P('section', None, 'tensor'), may hold values from -6 to 6
- later_grad: bfloat16 [32, 1, 512, 2304], P('section', None, 'tensor'), may hold values from -6 to 6
- attn_gain: bfloat16 [32, 2304], P('section'), may hold values from 0.5 to 1.5
- w_query: bfloat16 [32, 2304, 4096], P('section', None, 'tensor'), may hold values from -0.125 to 0.125
- w_key: bfloat16 [32, 2304, 2048], P('section', None, 'tensor'), may hold values from -0.125 to 0.125
- w_value: bfloat16 [32, 2304, 2048], P('section', None, 'tensor'), may hold values from -0.125 to 0.125
- w_out: bfloat16 [32, 4096, 2304], P('section', 'tensor'), may hold values from -0.09375 to 0.09375
- final_gain: bfloat16 [2304], replicated, may hold values from 0.5 to 1.5
- reward_head: bfloat16 [2304], replicated, may hold values from -0.125 to 0.125
- rankings: int32 [1, 8], replicated, may hold values from 0 to 7, each once within a row
- lengths: int32 [1, 8], replicated, may hold values from 1 to 64, as said below
Outputs:
- arrived: bfloat16 [32, 1, 512, 2304], P('section', None, 'tensor')
- sent_back: bfloat16 [32, 1, 512, 2304], P('section', None, 'tensor')
The draws below stay inside these ranges and needn't reach their ends.
Inputs may be any that keep to these rules, and one draw needn't show every extreme that they name: `rankings`: each row names every response once; entry j is the response ranked j-th best. `lengths`: each list has a response that fills all 64 slots.
All inputs are finite; a program needn't handle non-finite values.
Results may differ from the reference program's by a relative error of at most 0.04.
Values may be sent and summed in bfloat16 or wider, within the bound.
No kernel may reach another device: no remote copies, remote signals or barrier semaphores. Data moves between devices by JAX's collectives and lax.ppermute only.
A program may use at most 64 MiB of HBM per device.

```python
import jax
import jax.numpy as jnp
from jax import lax

D = 2304
HEADS = 32
KV_HEADS = 16
HEAD_DIM = 128
RESP = 8
RESP_LEN = 64
MICRO = 1
TOK = 512
SECTIONS = 32
N_TENSOR = 16


def draw_lengths(key, part):
    key = jax.random.fold_in(key, 7)
    first_key, second_key = jax.random.split(key)
    spread = jax.random.randint(first_key, (MICRO, RESP), 1, RESP_LEN + 1)
    filled = jax.random.randint(second_key, (MICRO, 1), 0, RESP)
    chosen = jnp.arange(RESP)[None, :] == filled
    return jnp.where(chosen, RESP_LEN, spread).astype(jnp.int32)


def level_of(stream_key, extent, cuts, least, largest):
    def one(position, shards_of):
        steps = jax.random.uniform(jax.random.fold_in(jax.random.fold_in(stream_key, 6), position), (shards_of,), jnp.float32, least / len(cuts), largest / len(cuts))
        return jnp.repeat(jnp.exp(steps), extent[position] // shards_of).reshape((-1,) + (1,) * (len(extent) - position - 1))

    factor_of = one(*cuts[0])
    for cut in cuts[1:]:
        factor_of = factor_of * one(*cut)
    return factor_of


def gaussian(key, dims, deviation, bound, cuts=(), dtype=jnp.bfloat16):
    level = level_of(key, dims, cuts, -0.22, 0.18) if cuts else 1.0
    result = jax.random.normal(key, dims, jnp.float32) * deviation * level
    return jnp.minimum(jnp.maximum(result, -bound), bound).astype(dtype)


def setup_inputs(seed: int = 0) -> dict:
    arg_keys = jax.random.split(jax.random.key(seed), 12)
    return {
        "section_inputs": gaussian(arg_keys[0], (SECTIONS, MICRO, TOK, D), 1.0, 6.0, ((0, 32), (2, 16))),
        "later_grad": gaussian(arg_keys[1], (SECTIONS, MICRO, TOK, D), 1.0, 6.0, ((0, 32), (2, 16))),
        "attn_gain": jnp.clip(1.0 + 0.1 * jax.random.normal(arg_keys[2], (SECTIONS, D), jnp.float32), 0.5, 1.5).astype(jnp.bfloat16),
        "w_query": gaussian(arg_keys[3], (SECTIONS, D, HEADS * HEAD_DIM), D ** -0.5, 0.125, ((0, 32), (2, 16))),
        "w_key": gaussian(arg_keys[4], (SECTIONS, D, KV_HEADS * HEAD_DIM), D ** -0.5, 0.125, ((0, 32), (2, 16))),
        "w_value": gaussian(arg_keys[5], (SECTIONS, D, KV_HEADS * HEAD_DIM), D ** -0.5, 0.125, ((0, 32), (2, 16))),
        "w_out": gaussian(arg_keys[6], (SECTIONS, HEADS * HEAD_DIM, D), (HEADS * HEAD_DIM) ** -0.5, 0.09375, ((0, 32), (1, 16))),
        "final_gain": jnp.clip(1.0 + 0.1 * jax.random.normal(arg_keys[7], (D,), jnp.float32), 0.5, 1.5).astype(jnp.bfloat16),
        "reward_head": gaussian(arg_keys[8], (D,), D ** -0.5, 0.125),
        "rankings": jax.vmap(lambda own: jax.random.permutation(own, RESP))(jax.random.split(arg_keys[9], MICRO)).reshape((MICRO, RESP)).astype(jnp.int32),
        "lengths": draw_lengths(jax.random.fold_in(arg_keys[11], 71), 0),
    }


EPSILON = 1e-06
SOFT_CAP = 50.0
QUERY_SCALE = 1.0 / 12.0
LOSS_SCALE = 64.0

def inv_rms(values):
    return lax.rsqrt(lax.optimization_barrier(jnp.mean(values * values, axis=-1, keepdims=True)) + EPSILON)

def causal_mask(length):
    places = jnp.arange(length)
    return (places[:, None] >= places[None, :]).astype(jnp.float32)

def attend(queries, key_row_block, value_rows, length):
    groups = key_row_block.shape[1] // HEAD_DIM
    q_split = queries.astype(jnp.float32).reshape(RESP, length, groups, 2, HEAD_DIM)
    k_split = key_row_block.astype(jnp.float32).reshape(RESP, length, groups, HEAD_DIM)
    v_split = value_rows.astype(jnp.float32).reshape(RESP, length, groups, HEAD_DIM)
    raw_score = jnp.einsum('rqgjd,rkgd->rgjqk', q_split, k_split, precision=lax.Precision.HIGHEST)
    capped = jnp.tanh(raw_score * (QUERY_SCALE / SOFT_CAP))
    exp_score = jnp.exp(SOFT_CAP * capped) * causal_mask(length)
    attn_prob = exp_score / lax.optimization_barrier(jnp.sum(exp_score, axis=-1, keepdims=True))
    prob_bf = attn_prob.astype(jnp.bfloat16)
    context = jnp.einsum('rgjqk,rkgd->rqgjd', prob_bf.astype(jnp.float32), v_split, precision=lax.Precision.HIGHEST)
    context = context.reshape(queries.shape[0], -1).astype(jnp.bfloat16)
    return (context, (capped, attn_prob, prob_bf))

def attend_back(grad_ctx, queries, key_row_block, value_rows, attn_state, length):
    capped, attn_prob, prob_bf = attn_state
    groups = key_row_block.shape[1] // HEAD_DIM
    q_split = queries.astype(jnp.float32).reshape(RESP, length, groups, 2, HEAD_DIM)
    k_split = key_row_block.astype(jnp.float32).reshape(RESP, length, groups, HEAD_DIM)
    v_split = value_rows.astype(jnp.float32).reshape(RESP, length, groups, HEAD_DIM)
    context_split = grad_ctx.astype(jnp.float32).reshape(RESP, length, groups, 2, HEAD_DIM)
    grad_prob = jnp.einsum('rqgjd,rkgd->rgjqk', context_split, v_split, precision=lax.Precision.HIGHEST)
    grad_score = attn_prob * (grad_prob - lax.optimization_barrier(jnp.sum(attn_prob * grad_prob, axis=-1, keepdims=True)))
    grad_raw = (grad_score * (1.0 - capped * capped) * QUERY_SCALE).astype(jnp.bfloat16).astype(jnp.float32)
    total_rows = queries.shape[0]
    grad_query = jnp.einsum('rgjqk,rkgd->rqgjd', grad_raw, k_split, precision=lax.Precision.HIGHEST)
    grad_key = jnp.einsum('rgjqk,rqgjd->rkgd', grad_raw, q_split, precision=lax.Precision.HIGHEST)
    grad_value = jnp.einsum('rgjqk,rqgjd->rkgd', prob_bf.astype(jnp.float32), context_split, precision=lax.Precision.HIGHEST)
    return (grad_query.reshape(total_rows, -1).astype(jnp.bfloat16), grad_key.reshape(total_rows, -1).astype(jnp.bfloat16), grad_value.reshape(total_rows, -1).astype(jnp.bfloat16))

def group_terms(left_mat, right_mat):
    total_rows = left_mat.shape[0]
    left_split = left_mat.astype(jnp.float32).reshape(total_rows, N_TENSOR, -1)
    right_split = right_mat.astype(jnp.float32).reshape(N_TENSOR, -1, right_mat.shape[1])
    return jnp.einsum('tgc,gcd->gtd', left_split, right_split, precision=lax.Precision.HIGHEST)

def round_sum(terms):
    rounded = lax.optimization_barrier(terms.astype(jnp.bfloat16))
    return lax.optimization_barrier(jnp.sum(rounded.astype(jnp.float32), axis=0))

def project(inputs_row, norm_gain, query_w, key_w, value_w):
    x_float = inputs_row.astype(jnp.float32)
    normed = (x_float * inv_rms(x_float) * norm_gain.astype(jnp.float32)).astype(jnp.bfloat16)
    queries = jnp.dot(normed, query_w, preferred_element_type=jnp.float32).astype(jnp.bfloat16)
    key_row_block = jnp.dot(normed, key_w, preferred_element_type=jnp.float32).astype(jnp.bfloat16)
    value_rows = jnp.dot(normed, value_w, preferred_element_type=jnp.float32).astype(jnp.bfloat16)
    return (queries, key_row_block, value_rows)

def layer_forward(packed):
    inputs, norm_gain, query_w, key_w, value_w, out_w = packed
    length = inputs.shape[1] // RESP
    outputs = []
    for micro_idx in range(MICRO):
        queries, key_row_block, value_rows = project(inputs[micro_idx], norm_gain, query_w, key_w, value_w)
        context, attn_state = attend(queries, key_row_block, value_rows, length)
        mixed = round_sum(group_terms(context, out_w))
        outputs.append((inputs[micro_idx].astype(jnp.float32) + mixed).astype(jnp.bfloat16))
    return jnp.stack(outputs)

def layer_backward(packed):
    inputs, cotangent, norm_gain, query_w, key_w, value_w, out_w = packed
    length = inputs.shape[1] // RESP
    gain_float = norm_gain.astype(jnp.float32)
    returned = []
    for micro_idx in range(MICRO):
        queries, key_row_block, value_rows = project(inputs[micro_idx], norm_gain, query_w, key_w, value_w)
        context, attn_state = attend(queries, key_row_block, value_rows, length)
        grad_own = cotangent[micro_idx]
        grad_ctx = jnp.dot(grad_own, out_w.T, preferred_element_type=jnp.float32).astype(jnp.bfloat16)
        grad_query, grad_key, grad_value = attend_back(grad_ctx, queries, key_row_block, value_rows, attn_state, length)
        terms = group_terms(grad_query, query_w.T) + group_terms(grad_key, key_w.T) + group_terms(grad_value, value_w.T)
        back_rows = round_sum(terms)
        x_float = inputs[micro_idx].astype(jnp.float32)
        inv_x = inv_rms(x_float)
        scaled_x = back_rows * gain_float
        grad_x = inv_x * scaled_x - x_float * inv_x ** 3 * lax.optimization_barrier(jnp.mean(scaled_x * x_float, axis=-1, keepdims=True))
        returned.append((grad_own.astype(jnp.float32) + grad_x).astype(jnp.bfloat16))
    return jnp.stack(returned)

def rank_grad(reward_scores, rankings):
    slots = jnp.arange(RESP)
    order_hot = (rankings[:, :, None] == slots[None, None, :]).astype(jnp.float32)
    ordered = jnp.einsum('mji,mi->mj', order_hot, reward_scores, precision=lax.Precision.HIGHEST)
    exp_order = jnp.exp(ordered)
    upper = (slots[:, None] >= slots[None, :]).astype(jnp.float32)
    suffix = jnp.dot(exp_order, upper, precision=lax.Precision.HIGHEST)
    cumulative = jnp.dot(1.0 / suffix, upper.T, precision=lax.Precision.HIGHEST)
    grad_order = LOSS_SCALE / MICRO * (exp_order * cumulative - 1.0)
    return jnp.einsum('mji,mj->mi', order_hot, grad_order, precision=lax.Precision.HIGHEST)

def reference(section_inputs, later_grad, attn_gain, w_query, w_key, w_value, w_out, final_gain, reward_head, rankings, lengths):
    hidden = lax.map(layer_forward, (section_inputs, attn_gain, w_query, w_key, w_value, w_out))
    last_hidden = hidden[-1]
    total_rows = last_hidden.shape[1]
    length = total_rows // RESP
    hidden_f = last_hidden.astype(jnp.float32)
    inv_norm = inv_rms(hidden_f)
    head_vec = final_gain.astype(jnp.float32) * reward_head.astype(jnp.float32)
    score_per_row = lax.optimization_barrier(jnp.sum(hidden_f * inv_norm * head_vec, axis=-1))
    positions = (jnp.arange(RESP)[None, :] * length + lengths - 1).astype(jnp.int32)
    selection_onehot = (positions[:, :, None] == jnp.arange(total_rows).astype(jnp.int32)[None, None, :]).astype(jnp.float32)
    reward_scores = jnp.einsum('hgn,hn->hg', selection_onehot, score_per_row, precision=lax.Precision.HIGHEST)
    gradient_of_scores = rank_grad(reward_scores, rankings)
    gradient_per_row = jnp.einsum('jsc,js->jc', selection_onehot, gradient_of_scores, precision=lax.Precision.HIGHEST)
    scaled = gradient_per_row[:, :, None] * head_vec
    last_grad = inv_norm * scaled - hidden_f * inv_norm ** 3 * lax.optimization_barrier(jnp.mean(scaled * hidden_f, axis=-1, keepdims=True))
    last_grad = last_grad.astype(jnp.bfloat16)
    cotangent = jnp.concatenate([later_grad[:-1], last_grad[None]], axis=0)
    returned = lax.map(layer_backward, (section_inputs, cotangent, attn_gain, w_query, w_key, w_value, w_out))
    arrived = jnp.concatenate([jnp.zeros_like(hidden[:1]), hidden[:-1]], axis=0)
    sent_back = jnp.concatenate([returned[1:], jnp.zeros_like(returned[:1])], axis=0)
    return (arrived, sent_back)
```

```python
import functools

import jax
import jax.numpy as jnp
from jax import lax
from jax.experimental import pallas as pl
from jax.experimental.pallas import tpu as pltpu
from jax.sharding import PartitionSpec as P

HEAD_DIM = 128
RESP = 8

EPSILON = 1e-06
SOFT_CAP = 50.0
QUERY_SCALE = 1.0 / 12.0
LOSS_SCALE = 64.0

F32 = jnp.float32
BF16 = jnp.bfloat16
VMEM_LIMIT = 48 * 1024 * 1024


def shift(value, steps):
    count = lax.axis_size("tensor")
    return lax.ppermute(value, "tensor", [(i, (i + steps) % count) for i in range(count)])


def from_behind(value, steps):
    count = lax.axis_size("section")
    leading, last = (max(0, -steps), min(count, count - steps))
    return lax.ppermute(value, "section", [(i, i + steps) for i in range(leading, last)])


def dot(left, right):
    return lax.dot_general(left, right, (((1,), (0,)), ((), ())), preferred_element_type=F32)


def dot_nt(left, right):
    return lax.dot_general(left, right, (((1,), (1,)), ((), ())), preferred_element_type=F32)


def dot_tn(left, right):
    return lax.dot_general(left, right, (((0,), (0,)), ((), ())), preferred_element_type=F32)


def inv_rms(values):
    return lax.rsqrt(jnp.mean(values * values, axis=-1, keepdims=True) + EPSILON)


def pair_mask(block, length):
    row = lax.broadcasted_iota(jnp.int32, (block, block), 0)
    col = lax.broadcasted_iota(jnp.int32, (block, block), 1)
    return ((row // length == col // length) & (col <= row)).astype(F32)


def row_picks(positions, rows):
    return (positions == lax.broadcasted_iota(jnp.int32, (RESP, rows), 1)).astype(BF16)


def attention(query, keys, mask):
    capped = jnp.tanh(dot_nt(query, keys) * (QUERY_SCALE / SOFT_CAP))
    exp_score = jnp.exp(SOFT_CAP * capped) * mask
    prob = exp_score / jnp.sum(exp_score, axis=-1, keepdims=True)
    return capped, prob


def forward_kernel(
    offsets, length, me_ref, positions_ref, gain_ref, wq_ref, wk_ref, wv_ref, wo_ref, *refs
):
    count = len(offsets)
    chunks = refs[:count]
    qkv_ref, mixed_ref, rows_x_ref, rows_m_ref, x_all, normed, context = refs[count:]
    own, feats = chunks[0].shape
    rows = own * count
    gain = gain_ref[...].astype(F32)
    for offset, chunk in zip(offsets, chunks):
        place = pl.multiple_of(lax.rem(me_ref[0] + (offset + count), count) * own, own)
        x = chunk[...]
        x_float = x.astype(F32)
        x_all[pl.ds(place, own), :] = x
        normed[pl.ds(place, own), :] = (x_float * inv_rms(x_float) * gain).astype(BF16)
    q_cols, kv_cols = wq_ref.shape[1], wk_ref.shape[1]
    qkv_ref[:, :q_cols] = dot(normed[...], wq_ref[...]).astype(BF16)
    qkv_ref[:, q_cols : q_cols + kv_cols] = dot(normed[...], wk_ref[...]).astype(BF16)
    qkv_ref[:, q_cols + kv_cols :] = dot(normed[...], wv_ref[...]).astype(BF16)
    block = 2 * length
    mask = pair_mask(block, length)
    for start in range(0, rows, block):
        span = slice(start, start + block)
        keys = qkv_ref[span, q_cols : q_cols + kv_cols]
        values = qkv_ref[span, q_cols + kv_cols :]
        for col in range(0, q_cols, HEAD_DIM):
            _, prob = attention(qkv_ref[span, col : col + HEAD_DIM], keys, mask)
            context[span, col : col + HEAD_DIM] = dot(prob.astype(BF16), values).astype(BF16)
    tile = 256

    @pl.loop(0, feats // tile)
    def _(i):
        cols = pl.ds(pl.multiple_of(i * tile, tile), tile)
        mixed_ref[:, cols] = dot(context[...], wo_ref[:, cols]).astype(BF16)

    picks = row_picks(positions_ref[...], rows)
    rows_x_ref[...] = dot(picks, x_all[...])
    rows_m_ref[...] = dot(dot(picks, context[...]).astype(BF16), wo_ref[...])


def forward_part(me, positions, gain, weights, chunks, offsets, length):
    own, feats = chunks[0].shape
    rows = own * len(chunks)
    vmem = pl.BlockSpec(memory_space=pltpu.VMEM)
    smem = pl.BlockSpec(memory_space=pltpu.SMEM)
    cols = sum(w.shape[1] for w in weights[:3])
    return pl.pallas_call(
        functools.partial(forward_kernel, offsets, length),
        out_shape=(
            jax.ShapeDtypeStruct((rows, cols), BF16),
            jax.ShapeDtypeStruct((rows, feats), BF16),
            jax.ShapeDtypeStruct((RESP, feats), F32),
            jax.ShapeDtypeStruct((RESP, feats), F32),
        ),
        in_specs=[smem] + [vmem] * (6 + len(chunks)),
        out_specs=[vmem] * 4,
        scratch_shapes=[
            pltpu.VMEM((rows, feats), BF16),
            pltpu.VMEM((rows, feats), BF16),
            pltpu.VMEM((rows, weights[0].shape[1]), BF16),
        ],
        compiler_params=pltpu.CompilerParams(vmem_limit_bytes=VMEM_LIMIT),
        name="layer_forward",
    )(me, positions, gain, *weights, *chunks)


def backward_kernel(
    offsets,
    length,
    me_ref,
    positions_ref,
    row_grads_ref,
    cot_ref,
    qkv_ref,
    wq_ref,
    wk_ref,
    wv_ref,
    wo_ref,
    *refs,
):
    count = len(offsets)
    outs = refs[:count]
    grads, turned = refs[count:]
    own, feats = outs[0].shape
    rows = own * count
    q_cols, kv_cols = wq_ref.shape[1], wk_ref.shape[1]
    picks = row_picks(positions_ref[...], rows)
    gathered_ctx = dot_nt(cot_ref[...], wo_ref[...]).astype(BF16)
    few = dot_nt(row_grads_ref[...].astype(BF16), wo_ref[...]).astype(BF16)
    placed_ctx = dot_tn(picks, few).astype(BF16)
    grad_ctx = jnp.where(me_ref[1] == 1, placed_ctx, gathered_ctx)
    block = 2 * length
    mask = pair_mask(block, length)
    for start in range(0, rows, block):
        span = slice(start, start + block)
        keys = qkv_ref[span, q_cols : q_cols + kv_cols]
        values = qkv_ref[span, q_cols + kv_cols :]
        grad_key = jnp.zeros((block, kv_cols), F32)
        grad_value = jnp.zeros((block, kv_cols), F32)
        for col in range(0, q_cols, HEAD_DIM):
            query = qkv_ref[span, col : col + HEAD_DIM]
            ctx = grad_ctx[span, col : col + HEAD_DIM]
            capped, prob = attention(query, keys, mask)
            grad_prob = dot_nt(ctx, values)
            grad_score = prob * (grad_prob - jnp.sum(prob * grad_prob, axis=-1, keepdims=True))
            grad_raw = (grad_score * (1.0 - capped * capped) * QUERY_SCALE).astype(BF16)
            grads[span, col : col + HEAD_DIM] = dot(grad_raw, keys).astype(BF16)
            grad_key += dot_tn(grad_raw, query)
            grad_value += dot_tn(prob.astype(BF16), ctx)
        grads[span, q_cols : q_cols + kv_cols] = grad_key.astype(BF16)
        grads[span, q_cols + kv_cols :] = grad_value.astype(BF16)
    for i, offset in enumerate(offsets):
        place = pl.multiple_of(lax.rem(me_ref[0] + (offset + count), count) * own, own)
        turned[i * own : (i + 1) * own, :] = grads[pl.ds(place, own), :]
    tile = 256

    @pl.loop(0, feats // tile)
    def _(i):
        cols = pl.ds(pl.multiple_of(i * tile, tile), tile)
        back = (
            dot_nt(turned[:, :q_cols], wq_ref[cols, :])
            + dot_nt(turned[:, q_cols : q_cols + kv_cols], wk_ref[cols, :])
            + dot_nt(turned[:, q_cols + kv_cols :], wv_ref[cols, :])
        ).astype(BF16)
        for j, out in enumerate(outs):
            out[:, cols] = back[j * own : (j + 1) * own, :]


def backward_part(me, positions, row_grads, cotangent, qkv, weights, offsets, length):
    rows, feats = cotangent.shape
    own = rows // len(offsets)
    vmem = pl.BlockSpec(memory_space=pltpu.VMEM)
    smem = pl.BlockSpec(memory_space=pltpu.SMEM)
    return pl.pallas_call(
        functools.partial(backward_kernel, offsets, length),
        out_shape=[jax.ShapeDtypeStruct((own, feats), BF16)] * len(offsets),
        in_specs=[smem] + [vmem] * 8,
        out_specs=[vmem] * len(offsets),
        scratch_shapes=[pltpu.VMEM(qkv.shape, BF16), pltpu.VMEM(qkv.shape, BF16)],
        compiler_params=pltpu.CompilerParams(vmem_limit_bytes=VMEM_LIMIT),
        name="layer_backward",
    )(me, positions, row_grads, cotangent, qkv, *weights)


def rank_grad(reward_scores, rankings):
    slots = jnp.arange(RESP)
    order_hot = (rankings[0][:, None] == slots[None, :]).astype(F32)
    ordered = jnp.sum(order_hot * reward_scores[None, :], axis=1)
    exp_order = jnp.exp(ordered)
    upper = (slots[:, None] >= slots[None, :]).astype(F32)
    suffix = jnp.sum(exp_order[:, None] * upper, axis=0)
    cumulative = jnp.sum((1.0 / suffix)[None, :] * upper, axis=1)
    grad_order = LOSS_SCALE * (exp_order * cumulative - 1.0)
    return jnp.sum(order_hot * grad_order[:, None], axis=0)


def gather_ring(block):
    count = lax.axis_size("tensor")
    blocks, offsets = [block], [0]
    up = down = block
    for step in range(1, count // 2 + 1):
        up = shift(up, 1)
        blocks.append(up)
        offsets.append(-step)
        if step < count - count // 2:
            down = shift(down, -1)
            blocks.append(down)
            offsets.append(step)
    return blocks, offsets


def scatter_ring(terms):
    count = lax.axis_size("tensor")
    half = count // 2
    up = terms[half]
    down = terms[-(count - half - 1)]
    for step in range(half):
        left = half - step - 1
        up = shift(up, 1)
        if left:
            up = (up.astype(F32) + terms[left].astype(F32)).astype(BF16)
        if left:
            down = shift(down, -1)
            if left > 1:
                down = (down.astype(F32) + terms[1 - left].astype(F32)).astype(BF16)
    return up, down


def sum_rows(value):
    step = 1
    while step < lax.axis_size("tensor"):
        value = value + shift(value, step)
        step *= 2
    return value


def shards(
    section_inputs,
    later_grad,
    attn_gain,
    w_query,
    w_key,
    w_value,
    w_out,
    final_gain,
    reward_head,
    rankings,
    lengths,
):
    x_own = section_inputs[0, 0]
    later_own = later_grad[0, 0]
    own_count = x_own.shape[0]
    tensor_count = lax.axis_size("tensor")
    tensor_pos = lax.axis_index("tensor")
    total_rows = own_count * tensor_count
    length = total_rows // RESP
    weights = (w_query[0], w_key[0], w_value[0], w_out[0])
    at_end = lax.axis_index("section") == lax.axis_size("section") - 1
    positions = jnp.arange(RESP) * length + lengths[0] - 1
    places = positions[:, None].astype(jnp.int32)
    me = jnp.stack([tensor_pos, at_end.astype(jnp.int32)])

    later_all = lax.all_gather(later_own, "tensor", axis=0, tiled=True)
    chunks, offsets = gather_ring(x_own)
    qkv, mixed, rows_x, rows_mixed = forward_part(
        me, places, attn_gain, weights, chunks, offsets, length
    )
    mixed_own = lax.psum_scatter(mixed, "tensor", scatter_dimension=0, tiled=True)

    rows_hidden = (rows_x + sum_rows(rows_mixed)).astype(BF16).astype(F32)
    inv_norm = inv_rms(rows_hidden)
    head_vec = final_gain.astype(F32) * reward_head.astype(F32)
    reward_scores = jnp.sum(rows_hidden * inv_norm * head_vec, axis=-1)
    scaled = rank_grad(reward_scores, rankings)[:, None] * head_vec
    row_grads = inv_norm * scaled - rows_hidden * inv_norm**3 * jnp.mean(
        scaled * rows_hidden, axis=-1, keepdims=True
    )
    row_grads = row_grads.astype(BF16).astype(F32)

    back_offsets = list(range(-(tensor_count - tensor_count // 2 - 1), tensor_count // 2 + 1))
    back = backward_part(
        me, places, row_grads, later_all, qkv, weights, back_offsets, length
    )
    terms = dict(zip(back_offsets, back))
    up, down = scatter_ring(terms)
    back_own = terms[0].astype(F32) + up.astype(F32) + down.astype(F32)

    own_rows = tensor_pos * own_count + jnp.arange(own_count)
    own_picks = (own_rows[:, None] == positions[None, :]).astype(F32)
    last_own = jnp.sum(own_picks[:, :, None] * row_grads[None], axis=1)
    grad_own = jnp.where(at_end, last_own, later_own.astype(F32))
    x_float = x_own.astype(F32)
    inv_x = inv_rms(x_float)
    scaled_x = back_own * attn_gain[0].astype(F32)
    grad_x = inv_x * scaled_x - x_float * inv_x**3 * jnp.mean(
        scaled_x * x_float, axis=-1, keepdims=True
    )
    returned = (grad_own + grad_x).astype(BF16)
    sent_back = from_behind(returned, -1)
    hidden = (x_float + mixed_own.astype(F32)).astype(BF16)
    arrived = from_behind(hidden, 1)
    return (arrived[None, None], sent_back[None, None])


def solution(mesh):
    return jax.shard_map(
        shards,
        mesh=mesh,
        in_specs=(
            P("section", None, "tensor", None),
            P("section", None, "tensor", None),
            P("section", None),
            P("section", None, "tensor"),
            P("section", None, "tensor"),
            P("section", None, "tensor"),
            P("section", "tensor", None),
            P(),
            P(),
            P(),
            P(),
        ),
        out_specs=(P("section", None, "tensor", None), P("section", None, "tensor", None)),
        check_vma=False,
    )
```

```python
import functools

import jax
import jax.numpy as jnp
from jax import lax
from jax.experimental import pallas as pl
from jax.experimental.pallas import tpu as pltpu
from jax.sharding import PartitionSpec as P

HEAD_DIM = 128
RESP = 8

EPSILON = 1e-06
SOFT_CAP = 50.0
QUERY_SCALE = 1.0 / 12.0
LOSS_SCALE = 64.0

F32 = jnp.float32
BF16 = jnp.bfloat16
VMEM_LIMIT = 24 * 1024 * 1024


def shift(value, steps, sections=None):
    count = lax.axis_size("tensor")
    sections = range(lax.axis_size("section")) if sections is None else sections
    pairs = [(s * count + i, s * count + (i + steps) % count) for s in sections for i in range(count)]
    return lax.ppermute(value, ("section", "tensor"), pairs)


def from_behind(value, steps):
    count = lax.axis_size("section")
    leading, last = (max(0, -steps), min(count, count - steps))
    return lax.ppermute(value, "section", [(i, i + steps) for i in range(leading, last)])


def dot(left, right):
    return lax.dot_general(left, right, (((1,), (0,)), ((), ())), preferred_element_type=F32)


def dot_nt(left, right):
    return lax.dot_general(left, right, (((1,), (1,)), ((), ())), preferred_element_type=F32)


def dot_tn(left, right):
    return lax.dot_general(left, right, (((0,), (0,)), ((), ())), preferred_element_type=F32)


def inv_rms(values):
    return lax.rsqrt(jnp.mean(values * values, axis=-1, keepdims=True) + EPSILON)


def pair_mask(block, length):
    row = lax.broadcasted_iota(jnp.int32, (block, block), 0)
    col = lax.broadcasted_iota(jnp.int32, (block, block), 1)
    return ((row // length == col // length) & (col <= row)).astype(F32)


def row_picks(positions, rows):
    return (positions == lax.broadcasted_iota(jnp.int32, (RESP, rows), 1)).astype(BF16)


def attention(queries, keys, mask):
    raw = [dot_nt(q, k) for q, k in zip(queries, keys)]
    capped = [jnp.tanh(r * (QUERY_SCALE / SOFT_CAP)) for r in raw]
    exps = [jnp.exp(SOFT_CAP * c) * mask for c in capped]
    sums = [jnp.sum(e, axis=-1, keepdims=True) for e in exps]
    return capped, [e / s for e, s in zip(exps, sums)]


def forward_kernel(
    offsets, length, me_ref, positions_ref, gain_ref, wq_ref, wk_ref, wv_ref, wo_ref, *refs
):
    blocks, (qkv_ref, mixed_ref, rows_ref, context) = refs[: len(offsets)], refs[len(offsets) :]
    count = sum(len(distances) for distances in offsets)
    rows, feats = mixed_ref.shape
    own = rows // count
    chunks = [b.at[i * own : (i + 1) * own] for b, d in zip(blocks, offsets) for i in range(len(d))]
    offsets = [distance for distances in offsets for distance in distances]
    gain = gain_ref[...].astype(F32)
    q_cols, kv_cols = wq_ref.shape[1], wk_ref.shape[1]
    w_kv = jnp.concatenate([wk_ref[...], wv_ref[...]], axis=1)
    batch = 4
    for first in range(0, count, batch):
        normed = []
        for chunk in chunks[first : first + batch]:
            x_float = chunk[...].astype(F32)
            normed.append((x_float * inv_rms(x_float) * gain).astype(BF16))
        normed = jnp.concatenate(normed, axis=0)
        q_part = dot(normed, wq_ref[...]).astype(BF16)
        kv_part = dot(normed, w_kv).astype(BF16)
        for i, offset in enumerate(offsets[first : first + batch]):
            place = pl.multiple_of(lax.rem(me_ref[0] + (offset + count), count) * own, own)
            span = slice(i * own, (i + 1) * own)
            qkv_ref[pl.ds(place, own), :q_cols] = q_part[span]
            qkv_ref[pl.ds(place, own), q_cols:] = kv_part[span]
    block = 2 * length
    mask = pair_mask(block, length)
    spans = [slice(start, start + block) for start in range(0, rows, block)]
    heads = range(0, q_cols, HEAD_DIM)
    queries = [qkv_ref[s, h : h + HEAD_DIM] for s in spans for h in heads]
    keys = [qkv_ref[s, q_cols : q_cols + kv_cols] for s in spans for h in heads]
    values = [qkv_ref[s, q_cols + kv_cols :] for s in spans for h in heads]
    _, probs = attention(queries, keys, mask)
    mixes = [dot(p.astype(BF16), v).astype(BF16) for p, v in zip(probs, values)]
    for i, (s, h) in enumerate((s, h) for s in spans for h in heads):
        context[s, h : h + HEAD_DIM] = mixes[i]
    for start in range(0, feats, 256):
        cols = slice(start, start + 256)
        mixed_ref[:, cols] = dot(context[...], wo_ref[:, cols]).astype(BF16)
    picks = row_picks(positions_ref[...], rows)
    own_picks = row_picks(positions_ref[...] - me_ref[0] * own, own)
    rows_ref[...] = dot(dot(picks, context[...]).astype(BF16), wo_ref[...]) + dot(
        own_picks, chunks[offsets.index(0)][...]
    )


def forward_part(me, positions, gain, weights, blocks, offsets, length):
    rows, feats = sum(b.shape[0] for b in blocks), blocks[0].shape[1]
    vmem = pl.BlockSpec(memory_space=pltpu.VMEM)
    smem = pl.BlockSpec(memory_space=pltpu.SMEM)
    cols = sum(w.shape[1] for w in weights[:3])
    return pl.pallas_call(
        functools.partial(forward_kernel, offsets, length),
        out_shape=(
            jax.ShapeDtypeStruct((rows, cols), BF16),
            jax.ShapeDtypeStruct((rows, feats), BF16),
            jax.ShapeDtypeStruct((RESP, feats), F32),
        ),
        in_specs=[smem] + [vmem] * (6 + len(blocks)),
        out_specs=[vmem] * 3,
        scratch_shapes=[pltpu.VMEM((rows, weights[0].shape[1]), BF16)],
        compiler_params=pltpu.CompilerParams(vmem_limit_bytes=VMEM_LIMIT),
        name="layer_forward",
    )(me, positions, gain, *weights, *blocks)


def backward_kernel(
    offsets,
    length,
    me_ref,
    positions_ref,
    row_grads_ref,
    cot_ref,
    qkv_ref,
    wq_ref,
    wk_ref,
    wv_ref,
    wo_ref,
    *refs,
):
    count = len(offsets)
    outs = refs[:count]
    grads, turned = refs[count:]
    own, feats = outs[0].shape
    rows = own * count
    q_cols, kv_cols = wq_ref.shape[1], wk_ref.shape[1]
    picks = row_picks(positions_ref[...], rows)
    gathered_ctx = dot_nt(cot_ref[...], wo_ref[...]).astype(BF16)
    few = dot_nt(row_grads_ref[...].astype(BF16), wo_ref[...]).astype(BF16)
    placed_ctx = dot_tn(picks, few).astype(BF16)
    grad_ctx = jnp.where(me_ref[1] == 1, placed_ctx, gathered_ctx)
    block = 2 * length
    mask = pair_mask(block, length)
    spans = [slice(start, start + block) for start in range(0, rows, block)]
    heads = range(0, q_cols, HEAD_DIM)
    pairs = [(s, h) for s in spans for h in heads]
    queries = [qkv_ref[s, h : h + HEAD_DIM] for s, h in pairs]
    keys = [qkv_ref[s, q_cols : q_cols + kv_cols] for s, h in pairs]
    values = [qkv_ref[s, q_cols + kv_cols :] for s, h in pairs]
    ctxs = [grad_ctx[s, h : h + HEAD_DIM] for s, h in pairs]
    capped, probs = attention(queries, keys, mask)
    grad_probs = [dot_nt(c, v) for c, v in zip(ctxs, values)]
    means = [jnp.sum(p * g, axis=-1, keepdims=True) for p, g in zip(probs, grad_probs)]
    raws = [
        (p * (g - m) * (1.0 - c * c) * QUERY_SCALE).astype(BF16)
        for p, g, m, c in zip(probs, grad_probs, means, capped)
    ]
    grad_queries = [dot(r, k).astype(BF16) for r, k in zip(raws, keys)]
    grad_keys = [dot_tn(r, q) for r, q in zip(raws, queries)]
    grad_values = [dot_tn(p.astype(BF16), c) for p, c in zip(probs, ctxs)]
    per = len(heads)
    for i, s in enumerate(spans):
        for j, h in enumerate(heads):
            grads[s, h : h + HEAD_DIM] = grad_queries[i * per + j]
        grads[s, q_cols : q_cols + kv_cols] = sum(grad_keys[i * per : (i + 1) * per]).astype(BF16)
        grads[s, q_cols + kv_cols :] = sum(grad_values[i * per : (i + 1) * per]).astype(BF16)
    for i, offset in enumerate(offsets):
        place = pl.multiple_of(lax.rem(me_ref[0] + (offset + count), count) * own, own)
        turned[i * own : (i + 1) * own, :] = grads[pl.ds(place, own), :]
    for start in range(0, feats, 256):
        cols = slice(start, start + 256)
        all_w = jnp.concatenate([wq_ref[cols, :], wk_ref[cols, :], wv_ref[cols, :]], axis=1)
        back = dot_nt(turned[...], all_w).astype(BF16)
        for j, out in enumerate(outs):
            out[:, cols] = back[j * own : (j + 1) * own, :]


def backward_part(me, positions, row_grads, cotangent, qkv, weights, offsets, length):
    rows, feats = cotangent.shape
    own = rows // len(offsets)
    vmem = pl.BlockSpec(memory_space=pltpu.VMEM)
    smem = pl.BlockSpec(memory_space=pltpu.SMEM)
    return pl.pallas_call(
        functools.partial(backward_kernel, offsets, length),
        out_shape=[jax.ShapeDtypeStruct((own, feats), BF16)] * len(offsets),
        in_specs=[smem] + [vmem] * 8,
        out_specs=[vmem] * len(offsets),
        scratch_shapes=[pltpu.VMEM(qkv.shape, BF16), pltpu.VMEM(qkv.shape, BF16)],
        compiler_params=pltpu.CompilerParams(vmem_limit_bytes=VMEM_LIMIT),
        name="layer_backward",
    )(me, positions, row_grads, cotangent, qkv, *weights)


def rank_grad(reward_scores, rankings):
    slots = jnp.arange(RESP)
    order_hot = (rankings[0][:, None] == slots[None, :]).astype(F32)
    ordered = jnp.sum(order_hot * reward_scores[None, :], axis=1)
    exp_order = jnp.exp(ordered)
    upper = (slots[:, None] >= slots[None, :]).astype(F32)
    suffix = jnp.sum(exp_order[:, None] * upper, axis=0)
    cumulative = jnp.sum((1.0 / suffix)[None, :] * upper, axis=1)
    grad_order = LOSS_SCALE * (exp_order * cumulative - 1.0)
    return jnp.sum(order_hot * grad_order[:, None], axis=0)


def gather_ring(block, sections):
    count = lax.axis_size("tensor")
    blocks, offsets = [block], [(0,)]
    up = down = block
    for step in range(1, count // 2 + 1):
        up = shift(up, 1, sections)
        blocks.append(up)
        offsets.append((-step,))
        if step < count - count // 2:
            down = shift(down, -1, sections)
            blocks.append(down)
            offsets.append((step,))
    return blocks, offsets


def gather_hops(block, sections):
    own = block.shape[0]
    far = jnp.concatenate([block, shift(block, 5, sections), shift(block, -5, sections)])
    left, right = shift(far, 1, sections), shift(far, -1, sections)
    left_on, right_on = shift(left, 1, sections), shift(right, -1, sections)
    across = shift(right[2 * own :], -2, sections)
    blocks = [far, left, right, left_on, right_on, across]
    offsets = [(0, -5, 5), (-1, -6, 4), (1, -4, 6), (-2, -7, 3), (2, -3, 7), (8,)]
    return blocks, offsets


def scatter_ring(terms):
    count = lax.axis_size("tensor")
    half = count // 2
    up = terms[half]
    down = terms[-(count - half - 1)]
    for step in range(half):
        left = half - step - 1
        up = shift(up, 1)
        if left:
            up = (up.astype(F32) + terms[left].astype(F32)).astype(BF16)
        if left:
            down = shift(down, -1)
            if left > 1:
                down = (down.astype(F32) + terms[1 - left].astype(F32)).astype(BF16)
    return up, down


def sum_rows(value, sections):
    step = 1
    while step < lax.axis_size("tensor"):
        value = value + shift(value, step, sections)
        step *= 2
    return value


def shards(
    section_inputs,
    later_grad,
    attn_gain,
    w_query,
    w_key,
    w_value,
    w_out,
    final_gain,
    reward_head,
    rankings,
    lengths,
):
    x_own = section_inputs[0, 0]
    later_own = later_grad[0, 0]
    own_count = x_own.shape[0]
    tensor_count = lax.axis_size("tensor")
    tensor_pos = lax.axis_index("tensor")
    total_rows = own_count * tensor_count
    length = total_rows // RESP
    weights = (w_query[0], w_key[0], w_value[0], w_out[0])
    at_end = lax.axis_index("section") == lax.axis_size("section") - 1
    positions = jnp.arange(RESP) * length + lengths[0] - 1
    places = positions[:, None].astype(jnp.int32)
    me = jnp.stack([tensor_pos, at_end.astype(jnp.int32)])

    later_all = lax.all_gather(later_own, "tensor", axis=0, tiled=True)
    last = lax.axis_size("section") - 1

    def forward(blocks, offsets):
        return forward_part(me, places, attn_gain, weights, blocks, offsets, length)

    def inner_section(x_own):
        qkv, mixed, rows_part = forward(*gather_ring(x_own, range(last)))
        return qkv, mixed, rows_part

    def last_section(x_own):
        qkv, mixed, rows_part = forward(*gather_hops(x_own, [last]))
        rows_hidden = sum_rows(rows_part, [last]).astype(BF16).astype(F32)
        inv_norm = inv_rms(rows_hidden)
        head_vec = final_gain.astype(F32) * reward_head.astype(F32)
        reward_scores = jnp.sum(rows_hidden * inv_norm * head_vec, axis=-1)
        scaled = rank_grad(reward_scores, rankings)[:, None] * head_vec
        row_grads = inv_norm * scaled - rows_hidden * inv_norm**3 * jnp.mean(
            scaled * rows_hidden, axis=-1, keepdims=True
        )
        return qkv, mixed, row_grads.astype(BF16).astype(F32)

    qkv, mixed, row_grads = lax.cond(at_end, last_section, inner_section, x_own)
    mixed_own = lax.psum_scatter(mixed, "tensor", scatter_dimension=0, tiled=True)

    back_offsets = list(range(-(tensor_count - tensor_count // 2 - 1), tensor_count // 2 + 1))
    back = backward_part(
        me, places, row_grads, later_all, qkv, weights, back_offsets, length
    )
    terms = dict(zip(back_offsets, back))
    up, down = scatter_ring(terms)
    back_own = terms[0].astype(F32) + up.astype(F32) + down.astype(F32)

    own_rows = tensor_pos * own_count + jnp.arange(own_count)
    own_picks = (own_rows[:, None] == positions[None, :]).astype(F32)
    last_own = jnp.sum(own_picks[:, :, None] * row_grads[None], axis=1)
    grad_own = jnp.where(at_end, last_own, later_own.astype(F32))
    x_float = x_own.astype(F32)
    inv_x = inv_rms(x_float)
    scaled_x = back_own * attn_gain[0].astype(F32)
    grad_x = inv_x * scaled_x - x_float * inv_x**3 * jnp.mean(
        scaled_x * x_float, axis=-1, keepdims=True
    )
    returned = (grad_own + grad_x).astype(BF16)
    sent_back = from_behind(returned, -1)
    hidden = (x_float + mixed_own.astype(F32)).astype(BF16)
    arrived = from_behind(hidden, 1)
    return (arrived[None, None], sent_back[None, None])


def solution(mesh):
    return jax.shard_map(
        shards,
        mesh=mesh,
        in_specs=(
            P("section", None, "tensor", None),
            P("section", None, "tensor", None),
            P("section", None),
            P("section", None, "tensor"),
            P("section", None, "tensor"),
            P("section", None, "tensor"),
            P("section", "tensor", None),
            P(),
            P(),
            P(),
            P(),
        ),
        out_specs=(P("section", None, "tensor", None), P("section", None, "tensor", None)),
        check_vma=False,
    )
```

```python
import functools

import jax
import jax.numpy as jnp
from jax import lax
from jax.experimental import pallas as pl
from jax.experimental.pallas import tpu as pltpu
from jax.sharding import PartitionSpec as P

HEAD_DIM = 128
RESP = 8

EPSILON = 1e-06
SOFT_CAP = 50.0
QUERY_SCALE = 1.0 / 12.0
LOSS_SCALE = 64.0

F32 = jnp.float32
BF16 = jnp.bfloat16
VMEM_LIMIT = 24 * 1024 * 1024


def shift(value, steps, sections=None):
    count = lax.axis_size("tensor")
    sections = range(lax.axis_size("section")) if sections is None else sections
    pairs = [(s * count + i, s * count + (i + steps) % count) for s in sections for i in range(count)]
    return lax.ppermute(value, ("section", "tensor"), pairs)


def from_behind(value, steps):
    count = lax.axis_size("section")
    leading, last = (max(0, -steps), min(count, count - steps))
    return lax.ppermute(value, "section", [(i, i + steps) for i in range(leading, last)])


def dot(left, right):
    return lax.dot_general(left, right, (((1,), (0,)), ((), ())), preferred_element_type=F32)


def dot_nt(left, right):
    return lax.dot_general(left, right, (((1,), (1,)), ((), ())), preferred_element_type=F32)


def dot_tn(left, right):
    return lax.dot_general(left, right, (((0,), (0,)), ((), ())), preferred_element_type=F32)


def inv_rms(values):
    return lax.rsqrt(jnp.mean(values * values, axis=-1, keepdims=True) + EPSILON)


def pair_mask(block, length):
    row = lax.broadcasted_iota(jnp.int32, (block, block), 0)
    col = lax.broadcasted_iota(jnp.int32, (block, block), 1)
    return ((row // length == col // length) & (col <= row)).astype(F32)


def row_picks(positions, rows):
    return (positions == lax.broadcasted_iota(jnp.int32, (RESP, rows), 1)).astype(BF16)


def attention(queries, keys, mask):
    raw = [dot_nt(q, k) for q, k in zip(queries, keys)]
    capped = [jnp.tanh(r * (QUERY_SCALE / SOFT_CAP)) for r in raw]
    exps = [jnp.exp(SOFT_CAP * c) * mask for c in capped]
    sums = [jnp.sum(e, axis=-1, keepdims=True) for e in exps]
    return capped, [e / s for e, s in zip(exps, sums)]


def forward_kernel(
    offsets, length, me_ref, positions_ref, gain_ref, wq_ref, wk_ref, wv_ref, wo_ref, *refs
):
    blocks, (qkv_ref, mixed_ref, rows_ref, context) = refs[: len(offsets)], refs[len(offsets) :]
    count = sum(len(distances) for distances in offsets)
    rows, feats = mixed_ref.shape
    own = rows // count
    chunks = [b.at[i * own : (i + 1) * own] for b, d in zip(blocks, offsets) for i in range(len(d))]
    offsets = [distance for distances in offsets for distance in distances]
    gain = gain_ref[...].astype(F32)
    q_cols, kv_cols = wq_ref.shape[1], wk_ref.shape[1]
    w_kv = jnp.concatenate([wk_ref[...], wv_ref[...]], axis=1)
    batch = 4
    for first in range(0, count, batch):
        normed = []
        for chunk in chunks[first : first + batch]:
            x_float = chunk[...].astype(F32)
            normed.append((x_float * inv_rms(x_float) * gain).astype(BF16))
        normed = jnp.concatenate(normed, axis=0)
        q_part = dot(normed, wq_ref[...]).astype(BF16)
        kv_part = dot(normed, w_kv).astype(BF16)
        for i, offset in enumerate(offsets[first : first + batch]):
            place = pl.multiple_of(lax.rem(me_ref[0] + (offset + count), count) * own, own)
            span = slice(i * own, (i + 1) * own)
            qkv_ref[pl.ds(place, own), :q_cols] = q_part[span]
            qkv_ref[pl.ds(place, own), q_cols:] = kv_part[span]
    block = 2 * length
    mask = pair_mask(block, length)
    spans = [slice(start, start + block) for start in range(0, rows, block)]
    heads = range(0, q_cols, HEAD_DIM)
    queries = [qkv_ref[s, h : h + HEAD_DIM] for s in spans for h in heads]
    keys = [qkv_ref[s, q_cols : q_cols + kv_cols] for s in spans for h in heads]
    values = [qkv_ref[s, q_cols + kv_cols :] for s in spans for h in heads]
    _, probs = attention(queries, keys, mask)
    mixes = [dot(p.astype(BF16), v).astype(BF16) for p, v in zip(probs, values)]
    for i, (s, h) in enumerate((s, h) for s in spans for h in heads):
        context[s, h : h + HEAD_DIM] = mixes[i]
    for start in range(0, feats, 256):
        cols = slice(start, start + 256)
        mixed_ref[:, cols] = dot(context[...], wo_ref[:, cols]).astype(BF16)
    picks = row_picks(positions_ref[...], rows)
    own_picks = row_picks(positions_ref[...] - me_ref[0] * own, own)
    rows_ref[...] = dot(dot(picks, context[...]).astype(BF16), wo_ref[...]) + dot(
        own_picks, chunks[offsets.index(0)][...]
    )


def forward_part(me, positions, gain, weights, blocks, offsets, length):
    rows, feats = sum(b.shape[0] for b in blocks), blocks[0].shape[1]
    vmem = pl.BlockSpec(memory_space=pltpu.VMEM)
    smem = pl.BlockSpec(memory_space=pltpu.SMEM)
    cols = sum(w.shape[1] for w in weights[:3])
    return pl.pallas_call(
        functools.partial(forward_kernel, offsets, length),
        out_shape=(
            jax.ShapeDtypeStruct((rows, cols), BF16),
            jax.ShapeDtypeStruct((rows, feats), BF16),
            jax.ShapeDtypeStruct((RESP, feats), F32),
        ),
        in_specs=[smem] + [vmem] * (6 + len(blocks)),
        out_specs=[vmem] * 3,
        scratch_shapes=[pltpu.VMEM((rows, weights[0].shape[1]), BF16)],
        compiler_params=pltpu.CompilerParams(vmem_limit_bytes=VMEM_LIMIT),
        name="layer_forward",
    )(me, positions, gain, *weights, *blocks)


def backward_kernel(
    offsets,
    length,
    me_ref,
    cot_ref,
    qkv_ref,
    wq_ref,
    wk_ref,
    wv_ref,
    wo_ref,
    *refs,
):
    count = len(offsets)
    outs = refs[:count]
    grads, turned = refs[count:]
    own, feats = outs[0].shape
    rows = own * count
    q_cols, kv_cols = wq_ref.shape[1], wk_ref.shape[1]
    grad_ctx = dot_nt(cot_ref[...], wo_ref[...]).astype(BF16)
    block = 2 * length
    mask = pair_mask(block, length)
    spans = [slice(start, start + block) for start in range(0, rows, block)]
    heads = range(0, q_cols, HEAD_DIM)
    pairs = [(s, h) for s in spans for h in heads]
    queries = [qkv_ref[s, h : h + HEAD_DIM] for s, h in pairs]
    keys = [qkv_ref[s, q_cols : q_cols + kv_cols] for s, h in pairs]
    values = [qkv_ref[s, q_cols + kv_cols :] for s, h in pairs]
    ctxs = [grad_ctx[s, h : h + HEAD_DIM] for s, h in pairs]
    capped, probs = attention(queries, keys, mask)
    grad_probs = [dot_nt(c, v) for c, v in zip(ctxs, values)]
    means = [jnp.sum(p * g, axis=-1, keepdims=True) for p, g in zip(probs, grad_probs)]
    raws = [
        (p * (g - m) * (1.0 - c * c) * QUERY_SCALE).astype(BF16)
        for p, g, m, c in zip(probs, grad_probs, means, capped)
    ]
    grad_queries = [dot(r, k).astype(BF16) for r, k in zip(raws, keys)]
    grad_keys = [dot_tn(r, q) for r, q in zip(raws, queries)]
    grad_values = [dot_tn(p.astype(BF16), c) for p, c in zip(probs, ctxs)]
    per = len(heads)
    for i, s in enumerate(spans):
        for j, h in enumerate(heads):
            grads[s, h : h + HEAD_DIM] = grad_queries[i * per + j]
        grads[s, q_cols : q_cols + kv_cols] = sum(grad_keys[i * per : (i + 1) * per]).astype(BF16)
        grads[s, q_cols + kv_cols :] = sum(grad_values[i * per : (i + 1) * per]).astype(BF16)
    for i, offset in enumerate(offsets):
        place = pl.multiple_of(lax.rem(me_ref[0] + (offset + count), count) * own, own)
        turned[i * own : (i + 1) * own, :] = grads[pl.ds(place, own), :]
    for start in range(0, feats, 256):
        cols = slice(start, start + 256)
        all_w = jnp.concatenate([wq_ref[cols, :], wk_ref[cols, :], wv_ref[cols, :]], axis=1)
        back = dot_nt(turned[...], all_w).astype(BF16)
        for j, out in enumerate(outs):
            out[:, cols] = back[j * own : (j + 1) * own, :]


def backward_part(me, cotangent, qkv, weights, offsets, length):
    rows, feats = cotangent.shape
    own = rows // len(offsets)
    vmem = pl.BlockSpec(memory_space=pltpu.VMEM)
    smem = pl.BlockSpec(memory_space=pltpu.SMEM)
    return pl.pallas_call(
        functools.partial(backward_kernel, offsets, length),
        out_shape=[jax.ShapeDtypeStruct((own, feats), BF16)] * len(offsets),
        in_specs=[smem] + [vmem] * 6,
        out_specs=[vmem] * len(offsets),
        scratch_shapes=[pltpu.VMEM(qkv.shape, BF16), pltpu.VMEM(qkv.shape, BF16)],
        compiler_params=pltpu.CompilerParams(vmem_limit_bytes=VMEM_LIMIT),
        name="layer_backward",
    )(me, cotangent, qkv, *weights)


def scored_kernel(
    count,
    length,
    positions_ref,
    row_grads_ref,
    qkv_ref,
    wq_ref,
    wk_ref,
    wv_ref,
    wo_ref,
    parcels_ref,
):
    rows = qkv_ref.shape[0]
    feats = wq_ref.shape[0]
    own = rows // count
    q_cols, kv_cols = wq_ref.shape[1], wk_ref.shape[1]
    positions = positions_ref[...]
    picks = row_picks(positions, rows)
    row = lax.broadcasted_iota(jnp.int32, (RESP, rows), 0)
    col = lax.broadcasted_iota(jnp.int32, (RESP, rows), 1)
    mask = ((col // length == row) & (col <= positions)).astype(F32)
    query_all = dot(picks, qkv_ref[:, :q_cols]).astype(BF16)
    ctx_all = dot_nt(row_grads_ref[...].astype(BF16), wo_ref[...]).astype(BF16)
    keys = qkv_ref[:, q_cols : q_cols + kv_cols]
    values = qkv_ref[:, q_cols + kv_cols :]
    heads = range(0, q_cols, HEAD_DIM)
    queries = [query_all[:, h : h + HEAD_DIM] for h in heads]
    ctxs = [ctx_all[:, h : h + HEAD_DIM] for h in heads]
    capped, probs = attention(queries, [keys] * len(heads), mask)
    raws = []
    for prob, cap, ctx in zip(probs, capped, ctxs):
        grad_prob = dot_nt(ctx, values)
        grad_score = prob * (grad_prob - jnp.sum(prob * grad_prob, axis=-1, keepdims=True))
        raws.append((grad_score * (1.0 - cap * cap) * QUERY_SCALE).astype(BF16))
    grad_query = jnp.concatenate([dot(raw, keys) for raw in raws], axis=1).astype(BF16)
    vectors = [dot_nt(q, wk_ref[...]) for q in queries] + [dot_nt(c, wv_ref[...]) for c in ctxs]
    vectors.append(dot_nt(grad_query, wq_ref[...]))
    fold_row = lax.broadcasted_iota(jnp.int32, (rows, length), 0)
    fold_col = lax.broadcasted_iota(jnp.int32, (rows, length), 1)
    fold = (fold_row % length == fold_col).astype(BF16)
    shares = [dot(c, fold) for c in raws + [p.astype(BF16) for p in probs] + [picks]]
    kinds = len(vectors)
    vectors = jnp.concatenate(vectors, axis=0).astype(BF16)
    shares = jnp.concatenate(shares, axis=0).astype(BF16)
    slots = parcels_ref.shape[0] // count
    out_row = lax.broadcasted_iota(jnp.int32, (count * slots, kinds * RESP), 0)
    source = lax.broadcasted_iota(jnp.int32, (count * slots, kinds * RESP), 1)
    owner, slot = out_row // slots, out_row % slots
    choose = ((slot == source // RESP) & (owner // (length // own) == source % RESP)).astype(BF16)
    parcels_ref[:, :feats] = dot(choose, vectors).astype(BF16)
    chosen = dot(choose, shares)
    half = (lax.broadcasted_iota(jnp.int32, (count * slots, own), 0) // slots) % (length // own)
    part = jnp.zeros((count * slots, own), F32)
    for i in range(length // own):
        part = jnp.where(half == i, chosen[:, i * own : (i + 1) * own], part)
    tail = jnp.zeros((count * slots, 128 - own), F32)
    parcels_ref[:, feats:] = jnp.concatenate([part, tail], axis=1).astype(BF16)


def scored_part(positions, row_grads, qkv, weights, count, length):
    feats = row_grads.shape[1]
    vmem = pl.BlockSpec(memory_space=pltpu.VMEM)
    slots = 8
    parcels = pl.pallas_call(
        functools.partial(scored_kernel, count, length),
        out_shape=jax.ShapeDtypeStruct((count * slots, feats + 128), BF16),
        in_specs=[vmem] * 7,
        out_specs=vmem,
        compiler_params=pltpu.CompilerParams(vmem_limit_bytes=VMEM_LIMIT),
        name="scored_backward",
    )(positions, row_grads, qkv, *weights)
    parcels = lax.all_to_all(parcels.reshape(count, slots, -1), "tensor", 0, 0)
    parcels = parcels.reshape(count * slots, -1)
    own = qkv.shape[0] // count
    return dot_tn(parcels[:, feats : feats + own], parcels[:, :feats])


def rank_grad(reward_scores, rankings):
    slots = jnp.arange(RESP)
    order_hot = (rankings[0][:, None] == slots[None, :]).astype(F32)
    ordered = jnp.sum(order_hot * reward_scores[None, :], axis=1)
    exp_order = jnp.exp(ordered)
    upper = (slots[:, None] >= slots[None, :]).astype(F32)
    suffix = jnp.sum(exp_order[:, None] * upper, axis=0)
    cumulative = jnp.sum((1.0 / suffix)[None, :] * upper, axis=1)
    grad_order = LOSS_SCALE * (exp_order * cumulative - 1.0)
    return jnp.sum(order_hot * grad_order[:, None], axis=0)


def gather_ring(block):
    count = lax.axis_size("tensor")
    blocks, offsets = [block], [(0,)]
    up = down = block
    for step in range(1, count // 2 + 1):
        up = shift(up, 1)
        blocks.append(up)
        offsets.append((-step,))
        if step < count - count // 2:
            down = shift(down, -1)
            blocks.append(down)
            offsets.append((step,))
    return blocks, offsets


def scatter_ring(terms, sections):
    count = lax.axis_size("tensor")
    half = count // 2
    up = terms[half]
    down = terms[-(count - half - 1)]
    for step in range(half):
        left = half - step - 1
        up = shift(up, 1, sections)
        if left:
            up = (up.astype(F32) + terms[left].astype(F32)).astype(BF16)
        if left:
            down = shift(down, -1, sections)
            if left > 1:
                down = (down.astype(F32) + terms[1 - left].astype(F32)).astype(BF16)
    return terms[0].astype(F32) + up.astype(F32) + down.astype(F32)


def sum_rows(value, sections):
    step = 1
    while step < lax.axis_size("tensor"):
        value = value + shift(value, step, sections)
        step *= 2
    return value


def shards(
    section_inputs,
    later_grad,
    attn_gain,
    w_query,
    w_key,
    w_value,
    w_out,
    final_gain,
    reward_head,
    rankings,
    lengths,
):
    x_own = section_inputs[0, 0]
    later_own = later_grad[0, 0]
    own_count = x_own.shape[0]
    tensor_count = lax.axis_size("tensor")
    tensor_pos = lax.axis_index("tensor")
    total_rows = own_count * tensor_count
    length = total_rows // RESP
    weights = (w_query[0], w_key[0], w_value[0], w_out[0])
    at_end = lax.axis_index("section") == lax.axis_size("section") - 1
    positions = jnp.arange(RESP) * length + lengths[0] - 1
    places = positions[:, None].astype(jnp.int32)
    me = tensor_pos[None].astype(jnp.int32)

    later_all = lax.all_gather(later_own, "tensor", axis=0, tiled=True)
    last = lax.axis_size("section") - 1
    blocks, offsets = gather_ring(x_own)
    qkv, mixed, rows_part = forward_part(me, places, attn_gain, weights, blocks, offsets, length)
    mixed_own = lax.psum_scatter(mixed, "tensor", scatter_dimension=0, tiled=True)

    def inner_section(later_all, qkv, rows_part):
        far = tensor_count // 2
        back_offsets = list(range(far + 1 - tensor_count, far + 1))
        back = backward_part(me, later_all, qkv, weights, back_offsets, length)
        return scatter_ring(dict(zip(back_offsets, back)), range(last)), jnp.zeros_like(rows_part)

    def last_section(later_all, qkv, rows_part):
        rows_hidden = sum_rows(rows_part, [last]).astype(BF16).astype(F32)
        inv_norm = inv_rms(rows_hidden)
        head_vec = final_gain.astype(F32) * reward_head.astype(F32)
        reward_scores = jnp.sum(rows_hidden * inv_norm * head_vec, axis=-1)
        scaled = rank_grad(reward_scores, rankings)[:, None] * head_vec
        row_grads = inv_norm * scaled - rows_hidden * inv_norm**3 * jnp.mean(
            scaled * rows_hidden, axis=-1, keepdims=True
        )
        row_grads = row_grads.astype(BF16).astype(F32)
        return scored_part(places, row_grads, qkv, weights, tensor_count, length), row_grads

    back_own, row_grads = lax.cond(
        at_end, last_section, inner_section, later_all, qkv, rows_part
    )

    own_rows = tensor_pos * own_count + jnp.arange(own_count)
    own_picks = (own_rows[:, None] == positions[None, :]).astype(F32)
    last_own = jnp.sum(own_picks[:, :, None] * row_grads[None], axis=1)
    grad_own = jnp.where(at_end, last_own, later_own.astype(F32))
    x_float = x_own.astype(F32)
    inv_x = inv_rms(x_float)
    scaled_x = back_own * attn_gain[0].astype(F32)
    grad_x = inv_x * scaled_x - x_float * inv_x**3 * jnp.mean(
        scaled_x * x_float, axis=-1, keepdims=True
    )
    returned = (grad_own + grad_x).astype(BF16)
    sent_back = from_behind(returned, -1)
    hidden = (x_float + mixed_own.astype(F32)).astype(BF16)
    arrived = from_behind(hidden, 1)
    return (arrived[None, None], sent_back[None, None])


def solution(mesh):
    return jax.shard_map(
        shards,
        mesh=mesh,
        in_specs=(
            P("section", None, "tensor", None),
            P("section", None, "tensor", None),
            P("section", None),
            P("section", None, "tensor"),
            P("section", None, "tensor"),
            P("section", None, "tensor"),
            P("section", "tensor", None),
            P(),
            P(),
            P(),
            P(),
        ),
        out_specs=(P("section", None, "tensor", None), P("section", None, "tensor", None)),
        check_vma=False,
    )
```

```python
import functools

import jax
import jax.numpy as jnp
from jax import lax
from jax.experimental import pallas as pl
from jax.experimental.pallas import tpu as pltpu
from jax.sharding import PartitionSpec as P

HEAD_DIM = 128
RESP = 8

EPSILON = 1e-06
SOFT_CAP = 50.0
QUERY_SCALE = 1.0 / 12.0
LOSS_SCALE = 64.0

F32 = jnp.float32
BF16 = jnp.bfloat16
VMEM_LIMIT = 24 * 1024 * 1024
BATCH = 8
FIRST_TERMS = 2


def shift(value, steps, sections=None):
    count = lax.axis_size("tensor")
    sections = range(lax.axis_size("section")) if sections is None else sections
    pairs = [(s * count + i, s * count + (i + steps) % count) for s in sections for i in range(count)]
    return lax.ppermute(value, ("section", "tensor"), pairs)


def from_behind(value, steps):
    count = lax.axis_size("section")
    leading, last = (max(0, -steps), min(count, count - steps))
    return lax.ppermute(value, "section", [(i, i + steps) for i in range(leading, last)])


def dot(left, right):
    return lax.dot_general(left, right, (((1,), (0,)), ((), ())), preferred_element_type=F32)


def dot_nt(left, right):
    return lax.dot_general(left, right, (((1,), (1,)), ((), ())), preferred_element_type=F32)


def dot_tn(left, right):
    return lax.dot_general(left, right, (((0,), (0,)), ((), ())), preferred_element_type=F32)


def inv_rms(values):
    return lax.rsqrt(jnp.mean(values * values, axis=-1, keepdims=True) + EPSILON)


def pair_mask(block, length):
    row = lax.broadcasted_iota(jnp.int32, (block, block), 0)
    col = lax.broadcasted_iota(jnp.int32, (block, block), 1)
    return ((row // length == col // length) & (col <= row)).astype(F32)


def row_picks(positions, rows):
    return (positions == lax.broadcasted_iota(jnp.int32, (RESP, rows), 1)).astype(BF16)


def attention(queries, keys, mask):
    raw = [dot_nt(q, k) for q, k in zip(queries, keys)]
    capped = [jnp.tanh(r * (QUERY_SCALE / SOFT_CAP)) for r in raw]
    exps = [jnp.exp(SOFT_CAP * c) * mask for c in capped]
    sums = [jnp.sum(e, axis=-1, keepdims=True) for e in exps]
    return capped, [e / s for e, s in zip(exps, sums)]


def project(me_ref, gain_ref, wq_ref, wk_ref, wv_ref, wo_ref, blocks):
    own = blocks[0].shape[0] // 2
    gain = gain_ref[...].astype(F32)
    normed = []
    for block in blocks:
        x_float = block[:own].astype(F32)
        normed.append((x_float * inv_rms(x_float) * gain).astype(BF16))
    normed = jnp.concatenate(normed, axis=0)
    w_kv = jnp.concatenate([wk_ref[...], wv_ref[...]], axis=1)
    cot = jnp.concatenate([block[own:] for block in blocks], axis=0)
    parts = [dot(normed, wq_ref[...]), dot(normed, w_kv), dot_nt(cot, wo_ref[...])]
    return [part.astype(BF16) for part in parts]


def early_kernel(gain_ref, wq_ref, wk_ref, wv_ref, wo_ref, *refs):
    blocks, out_ref = refs[:-1], refs[-1]
    own = blocks[0].shape[0] // 2
    for first in range(0, len(blocks), BATCH):
        some = blocks[first : first + BATCH]
        parts = project(None, gain_ref, wq_ref, wk_ref, wv_ref, wo_ref, some)
        rows = slice(first * own, (first + len(some)) * own)
        out_ref[rows, :] = jnp.concatenate(parts, axis=1)


def early_part(gain, weights, blocks):
    own, feats = blocks[0].shape[0] // 2, blocks[0].shape[1]
    rows, cols = own * len(blocks), sum(w.shape[1] for w in weights[:3]) + weights[3].shape[0]
    vmem = pl.BlockSpec(memory_space=pltpu.VMEM)
    return pl.pallas_call(
        early_kernel,
        out_shape=jax.ShapeDtypeStruct((rows, cols), BF16),
        in_specs=[vmem] * (5 + len(blocks)),
        out_specs=vmem,
        compiler_params=pltpu.CompilerParams(vmem_limit_bytes=VMEM_LIMIT),
        cost_estimate=pl.CostEstimate(
            flops=2 * rows * cols * feats, bytes_accessed=4 * rows * feats, transcendentals=0
        ),
        name="early_rows",
    )(gain, *weights, *blocks)


def place_all(offsets, me_ref, early_ref, late, qkv_ref, grad_ctx=None):
    count = len(offsets)
    cols = qkv_ref.shape[1]
    own = qkv_ref.shape[0] // count
    for i, offset in enumerate(offsets[:-1]):
        rows = pl.ds(place_of(me_ref, offset, count, own), own)
        qkv_ref[rows, :] = early_ref[i * own : (i + 1) * own, :cols]
        if grad_ctx is not None:
            grad_ctx[rows, :] = early_ref[i * own : (i + 1) * own, cols:]
    rows = pl.ds(place_of(me_ref, offsets[-1], count, own), own)
    qkv_ref[rows, :] = jnp.concatenate(late[:2], axis=1)
    if grad_ctx is not None:
        grad_ctx[rows, :] = late[2]


def place_of(me_ref, offset, count, own):
    return pl.multiple_of(lax.rem(me_ref[0] + (offset + count), count) * own, own)


def pairs_of(qkv_ref, length, q_cols, kv_cols):
    block = 2 * length
    spans = [slice(start, start + block) for start in range(0, qkv_ref.shape[0], block)]
    pairs = [(s, h) for s in spans for h in range(0, q_cols, HEAD_DIM)]
    queries = [qkv_ref[s, h : h + HEAD_DIM] for s, h in pairs]
    keys = [qkv_ref[s, q_cols : q_cols + kv_cols] for s, h in pairs]
    values = [qkv_ref[s, q_cols + kv_cols :] for s, h in pairs]
    return spans, pairs, queries, keys, values


def rows_kernel(
    offsets,
    length,
    me_ref,
    positions_ref,
    gain_ref,
    wq_ref,
    wk_ref,
    wv_ref,
    wo_ref,
    early_ref,
    first_ref,
    late_ref,
    qkv_ref,
    rows_ref,
    context,
):
    own = qkv_ref.shape[0] // len(offsets)
    late = project(me_ref, gain_ref, wq_ref, wk_ref, wv_ref, wo_ref, [late_ref])
    place_all(offsets, me_ref, early_ref, late, qkv_ref)
    q_cols, kv_cols = wq_ref.shape[1], wk_ref.shape[1]
    _, pairs, queries, keys, values = pairs_of(qkv_ref, length, q_cols, kv_cols)
    _, probs = attention(queries, keys, pair_mask(2 * length, length))
    for (s, h), prob, value in zip(pairs, probs, values):
        context[s, h : h + HEAD_DIM] = dot(prob.astype(BF16), value).astype(BF16)
    picks = row_picks(positions_ref[...], qkv_ref.shape[0])
    own_picks = row_picks(positions_ref[...] - me_ref[0] * own, own)
    rows_ref[...] = dot(dot(picks, context[...]).astype(BF16), wo_ref[...]) + dot(
        own_picks, first_ref[:own]
    )


def rows_part_of(me, positions, gain, weights, early, first, late, offsets, length):
    own, feats = late.shape[0] // 2, late.shape[1]
    rows = own * len(offsets)
    vmem = pl.BlockSpec(memory_space=pltpu.VMEM)
    smem = pl.BlockSpec(memory_space=pltpu.SMEM)
    cols = sum(w.shape[1] for w in weights[:3])
    return pl.pallas_call(
        functools.partial(rows_kernel, offsets, length),
        out_shape=(
            jax.ShapeDtypeStruct((rows, cols), BF16),
            jax.ShapeDtypeStruct((RESP, feats), F32),
        ),
        in_specs=[smem] + [vmem] * 9,
        out_specs=[vmem] * 2,
        scratch_shapes=[pltpu.VMEM((rows, weights[0].shape[1]), BF16)],
        compiler_params=pltpu.CompilerParams(vmem_limit_bytes=VMEM_LIMIT),
        name="scored_rows",
    )(me, positions, gain, *weights, early, first, late)


def project_back(turned, wq_ref, wk_ref, wv_ref, wo_ref, outs):
    own, feats = outs[0].shape[0] // 2, outs[0].shape[1]
    at_mix = turned.shape[1] - wo_ref.shape[0]
    for start in range(0, feats, 256):
        cols = slice(start, start + 256)
        all_w = jnp.concatenate([wq_ref[cols, :], wk_ref[cols, :], wv_ref[cols, :]], axis=1)
        back = dot_nt(turned[:, :at_mix], all_w).astype(BF16)
        mixed = dot(turned[:, at_mix:], wo_ref[:, cols]).astype(BF16)
        for j, out in enumerate(outs):
            out[:own, cols] = mixed[j * own : (j + 1) * own]
            out[own:, cols] = back[j * own : (j + 1) * own]


def layer_kernel(
    offsets,
    back_offsets,
    length,
    me_ref,
    gain_ref,
    wq_ref,
    wk_ref,
    wv_ref,
    wo_ref,
    early_ref,
    late_ref,
    *refs,
):
    count = len(offsets)
    outs, rest_ref = refs[:FIRST_TERMS], refs[FIRST_TERMS]
    qkv, grad_ctx, work, first_rows = refs[FIRST_TERMS + 1 :]
    own = late_ref.shape[0] // 2
    q_cols, kv_cols = wq_ref.shape[1], wk_ref.shape[1]
    late = project(me_ref, gain_ref, wq_ref, wk_ref, wv_ref, wo_ref, [late_ref])
    place_all(offsets, me_ref, early_ref, late, qkv, grad_ctx)
    spans, pairs, queries, keys, values = pairs_of(qkv, length, q_cols, kv_cols)
    ctxs = [grad_ctx[s, h : h + HEAD_DIM] for s, h in pairs]
    capped, probs = attention(queries, keys, pair_mask(2 * length, length))
    grad_probs = [dot_nt(c, v) for c, v in zip(ctxs, values)]
    means = [jnp.sum(p * g, axis=-1, keepdims=True) for p, g in zip(probs, grad_probs)]
    raws = [
        (p * (g - m) * (1.0 - c * c) * QUERY_SCALE).astype(BF16)
        for p, g, m, c in zip(probs, grad_probs, means, capped)
    ]
    probs = [p.astype(BF16) for p in probs]
    mixes = [dot(p, v).astype(BF16) for p, v in zip(probs, values)]
    grad_queries = [dot(r, k).astype(BF16) for r, k in zip(raws, keys)]
    grad_keys = [dot_tn(r, q) for r, q in zip(raws, queries)]
    grad_values = [dot_tn(p, c) for p, c in zip(probs, ctxs)]
    per = q_cols // HEAD_DIM
    at_keys, at_values, at_mix = q_cols, q_cols + kv_cols, q_cols + 2 * kv_cols
    for (s, h), grad_query, mix in zip(pairs, grad_queries, mixes):
        work[s, h : h + HEAD_DIM] = grad_query
        work[s, at_mix + h : at_mix + h + HEAD_DIM] = mix
    for i, s in enumerate(spans):
        work[s, at_keys:at_values] = sum(grad_keys[i * per : (i + 1) * per]).astype(BF16)
        work[s, at_values:at_mix] = sum(grad_values[i * per : (i + 1) * per]).astype(BF16)
    for i, offset in enumerate(back_offsets):
        rows = work[pl.ds(place_of(me_ref, offset, count, own), own), :]
        if i < FIRST_TERMS:
            first_rows[i * own : (i + 1) * own, :] = rows
        else:
            rest_ref[(i - FIRST_TERMS) * own : (i - FIRST_TERMS + 1) * own, :] = rows
    project_back(first_rows, wq_ref, wk_ref, wv_ref, wo_ref, outs)


def rest_kernel(wq_ref, wk_ref, wv_ref, wo_ref, rest_ref, *outs):
    project_back(rest_ref, wq_ref, wk_ref, wv_ref, wo_ref, outs)


def layer_part(me, gain, weights, early, late, offsets, back_offsets, length):
    count = len(offsets)
    own, feats = late.shape[0] // 2, late.shape[1]
    rows = own * count
    vmem = pl.BlockSpec(memory_space=pltpu.VMEM)
    smem = pl.BlockSpec(memory_space=pltpu.SMEM)
    cols = sum(w.shape[1] for w in weights[:3])
    q_cols = weights[0].shape[1]
    left = count - FIRST_TERMS
    term = jax.ShapeDtypeStruct(late.shape, BF16)
    *first, rest = pl.pallas_call(
        functools.partial(layer_kernel, offsets, back_offsets, length),
        out_shape=[term] * FIRST_TERMS + [jax.ShapeDtypeStruct((own * left, cols + q_cols), BF16)],
        in_specs=[smem] + [vmem] * 7,
        out_specs=[vmem] * (FIRST_TERMS + 1),
        scratch_shapes=[
            pltpu.VMEM((rows, cols), BF16),
            pltpu.VMEM((rows, q_cols), BF16),
            pltpu.VMEM((rows, cols + q_cols), BF16),
            pltpu.VMEM((own * FIRST_TERMS, cols + q_cols), BF16),
        ],
        compiler_params=pltpu.CompilerParams(vmem_limit_bytes=VMEM_LIMIT),
        name="layer_both_ways",
    )(me, gain, *weights, early, late)
    others = pl.pallas_call(
        rest_kernel,
        out_shape=[term] * left,
        in_specs=[vmem] * 5,
        out_specs=[vmem] * left,
        compiler_params=pltpu.CompilerParams(vmem_limit_bytes=VMEM_LIMIT),
        cost_estimate=pl.CostEstimate(
            flops=2 * rows * (cols + q_cols) * feats, bytes_accessed=0, transcendentals=0
        ),
        name="rest_of_terms",
    )(*weights, rest)
    return dict(zip(back_offsets, [*first, *others]))


def scored_kernel(
    count,
    length,
    positions_ref,
    row_grads_ref,
    qkv_ref,
    wq_ref,
    wk_ref,
    wv_ref,
    wo_ref,
    parcels_ref,
):
    rows = qkv_ref.shape[0]
    feats = wq_ref.shape[0]
    own = rows // count
    q_cols, kv_cols = wq_ref.shape[1], wk_ref.shape[1]
    positions = positions_ref[...]
    picks = row_picks(positions, rows)
    row = lax.broadcasted_iota(jnp.int32, (RESP, rows), 0)
    col = lax.broadcasted_iota(jnp.int32, (RESP, rows), 1)
    mask = ((col // length == row) & (col <= positions)).astype(F32)
    query_all = dot(picks, qkv_ref[:, :q_cols]).astype(BF16)
    ctx_all = dot_nt(row_grads_ref[...].astype(BF16), wo_ref[...]).astype(BF16)
    keys = qkv_ref[:, q_cols : q_cols + kv_cols]
    values = qkv_ref[:, q_cols + kv_cols :]
    heads = range(0, q_cols, HEAD_DIM)
    queries = [query_all[:, h : h + HEAD_DIM] for h in heads]
    ctxs = [ctx_all[:, h : h + HEAD_DIM] for h in heads]
    capped, probs = attention(queries, [keys] * len(heads), mask)
    raws = []
    for prob, cap, ctx in zip(probs, capped, ctxs):
        grad_prob = dot_nt(ctx, values)
        grad_score = prob * (grad_prob - jnp.sum(prob * grad_prob, axis=-1, keepdims=True))
        raws.append((grad_score * (1.0 - cap * cap) * QUERY_SCALE).astype(BF16))
    grad_query = jnp.concatenate([dot(raw, keys) for raw in raws], axis=1).astype(BF16)
    vectors = [dot_nt(q, wk_ref[...]) for q in queries] + [dot_nt(c, wv_ref[...]) for c in ctxs]
    vectors.append(dot_nt(grad_query, wq_ref[...]))
    fold_row = lax.broadcasted_iota(jnp.int32, (rows, length), 0)
    fold_col = lax.broadcasted_iota(jnp.int32, (rows, length), 1)
    fold = (fold_row % length == fold_col).astype(BF16)
    shares = [dot(c, fold) for c in raws + [p.astype(BF16) for p in probs] + [picks]]
    kinds = len(vectors)
    vectors = jnp.concatenate(vectors, axis=0).astype(BF16)
    shares = jnp.concatenate(shares, axis=0).astype(BF16)
    slots = parcels_ref.shape[0] // count
    out_row = lax.broadcasted_iota(jnp.int32, (count * slots, kinds * RESP), 0)
    source = lax.broadcasted_iota(jnp.int32, (count * slots, kinds * RESP), 1)
    owner, slot = out_row // slots, out_row % slots
    choose = ((slot == source // RESP) & (owner // (length // own) == source % RESP)).astype(BF16)
    share = length // own
    half = (lax.broadcasted_iota(jnp.int32, (count * slots, 1), 0) // slots) % share
    width = feats // share
    lanes = jnp.zeros((count * slots, width), F32)
    chosen = dot(choose, shares)
    part = jnp.zeros((count * slots, own), F32)
    for i in range(share):
        lanes = jnp.where(half == i, dot(choose, vectors[:, i * width : (i + 1) * width]), lanes)
        part = jnp.where(half == i, chosen[:, i * own : (i + 1) * own], part)
    parcels_ref[:, :width] = lanes.astype(BF16)
    tail = jnp.zeros((count * slots, 128 - own), F32)
    parcels_ref[:, width:] = jnp.concatenate([part, tail], axis=1).astype(BF16)


def scored_part(positions, row_grads, qkv, weights, count, length, section):
    width = row_grads.shape[1] // 2
    own = qkv.shape[0] // count
    vmem = pl.BlockSpec(memory_space=pltpu.VMEM)
    slots = 8
    parcels = pl.pallas_call(
        functools.partial(scored_kernel, count, length),
        out_shape=jax.ShapeDtypeStruct((count * slots, width + 128), BF16),
        in_specs=[vmem] * 7,
        out_specs=vmem,
        compiler_params=pltpu.CompilerParams(vmem_limit_bytes=VMEM_LIMIT),
        name="scored_backward",
    )(positions, row_grads, qkv, *weights)
    parcels = lax.all_to_all(parcels.reshape(count, slots, -1), "tensor", 0, 0)
    parcels = parcels.reshape(count * slots, -1)
    vectors, shares = parcels[:, :width], parcels[:, width : width + own]
    swaps = [(section * count + i, section * count + (i ^ 1)) for i in range(count)]
    swapped = lax.ppermute(vectors, ("section", "tensor"), swaps)
    mine, theirs = dot_tn(shares, vectors), dot_tn(shares, swapped)
    second = lax.axis_index("tensor") % 2 == 1
    return jnp.concatenate(
        [jnp.where(second, theirs, mine), jnp.where(second, mine, theirs)], axis=1
    )


def rank_grad(reward_scores, rankings):
    slots = jnp.arange(RESP)
    order_hot = (rankings[0][:, None] == slots[None, :]).astype(F32)
    ordered = jnp.sum(order_hot * reward_scores[None, :], axis=1)
    exp_order = jnp.exp(ordered)
    upper = (slots[:, None] >= slots[None, :]).astype(F32)
    suffix = jnp.sum(exp_order[:, None] * upper, axis=0)
    cumulative = jnp.sum((1.0 / suffix)[None, :] * upper, axis=1)
    grad_order = LOSS_SCALE * (exp_order * cumulative - 1.0)
    return jnp.sum(order_hot * grad_order[:, None], axis=0)


def gather_ring(block):
    count = lax.axis_size("tensor")
    blocks, offsets = [block], [0]
    up = down = block
    for step in range(1, count // 2 + 1):
        up = shift(up, 1)
        blocks.append(up)
        offsets.append(-step)
        if step < count - count // 2:
            down = shift(down, -1)
            blocks.append(down)
            offsets.append(step)
    return blocks, offsets


def scatter_ring(terms, sections):
    count = lax.axis_size("tensor")
    half = count // 2
    up = terms[half]
    down = terms[-(count - half - 1)]
    for step in range(half):
        left = half - step - 1
        up = shift(up, 1, sections)
        if left:
            up = (up.astype(F32) + terms[left].astype(F32)).astype(BF16)
        if left:
            down = shift(down, -1, sections)
            if left > 1:
                down = (down.astype(F32) + terms[1 - left].astype(F32)).astype(BF16)
    return terms[0].astype(F32) + up.astype(F32) + down.astype(F32)


def sum_rows(value, sections):
    step = 1
    while step < lax.axis_size("tensor"):
        value = value + shift(value, step, sections)
        step *= 2
    return value


def shards(
    section_inputs,
    later_grad,
    attn_gain,
    w_query,
    w_key,
    w_value,
    w_out,
    final_gain,
    reward_head,
    rankings,
    lengths,
):
    x_own = section_inputs[0, 0]
    later_own = later_grad[0, 0]
    own_count = x_own.shape[0]
    tensor_count = lax.axis_size("tensor")
    tensor_pos = lax.axis_index("tensor")
    total_rows = own_count * tensor_count
    length = total_rows // RESP
    weights = (w_query[0], w_key[0], w_value[0], w_out[0])
    at_end = lax.axis_index("section") == lax.axis_size("section") - 1
    positions = jnp.arange(RESP) * length + lengths[0] - 1
    places = positions[:, None].astype(jnp.int32)
    me = tensor_pos[None].astype(jnp.int32)

    last = lax.axis_size("section") - 1
    blocks, offsets = gather_ring(jnp.concatenate([x_own, later_own]))
    far = tensor_count // 2
    back_offsets = [far, far + 1 - tensor_count]
    back_offsets += [o for o in range(back_offsets[1] + 1, far)]
    early = early_part(attn_gain, weights, blocks[:-1])
    first, late = blocks[0], blocks[-1]

    def inner_section(early, first, late):
        terms = layer_part(me, attn_gain, weights, early, late, offsets, back_offsets, length)
        sums = scatter_ring(terms, range(last))
        return sums, jnp.zeros((RESP, x_own.shape[1]), F32)

    def last_section(early, first, late):
        qkv, rows_part = rows_part_of(
            me, places, attn_gain, weights, early, first, late, offsets, length
        )
        rows_hidden = sum_rows(rows_part, [last]).astype(BF16).astype(F32)
        inv_norm = inv_rms(rows_hidden)
        head_vec = final_gain.astype(F32) * reward_head.astype(F32)
        reward_scores = jnp.sum(rows_hidden * inv_norm * head_vec, axis=-1)
        scaled = rank_grad(reward_scores, rankings)[:, None] * head_vec
        row_grads = inv_norm * scaled - rows_hidden * inv_norm**3 * jnp.mean(
            scaled * rows_hidden, axis=-1, keepdims=True
        )
        row_grads = row_grads.astype(BF16).astype(F32)
        back_own = scored_part(
            places, row_grads, qkv, weights, tensor_count, length, last
        )
        return jnp.concatenate([jnp.zeros_like(back_own), back_own]), row_grads

    sums, row_grads = lax.cond(at_end, last_section, inner_section, early, first, late)
    mixed_own, back_own = sums[:own_count], sums[own_count:]

    own_rows = tensor_pos * own_count + jnp.arange(own_count)
    own_picks = (own_rows[:, None] == positions[None, :]).astype(F32)
    last_own = jnp.sum(own_picks[:, :, None] * row_grads[None], axis=1)
    grad_own = jnp.where(at_end, last_own, later_own.astype(F32))
    x_float = x_own.astype(F32)
    inv_x = inv_rms(x_float)
    scaled_x = back_own * attn_gain[0].astype(F32)
    grad_x = inv_x * scaled_x - x_float * inv_x**3 * jnp.mean(
        scaled_x * x_float, axis=-1, keepdims=True
    )
    returned = (grad_own + grad_x).astype(BF16)
    sent_back = from_behind(returned, -1)
    hidden = (x_float + mixed_own).astype(BF16)
    arrived = from_behind(hidden, 1)
    return (arrived[None, None], sent_back[None, None])


def solution(mesh):
    return jax.shard_map(
        shards,
        mesh=mesh,
        in_specs=(
            P("section", None, "tensor", None),
            P("section", None, "tensor", None),
            P("section", None),
            P("section", None, "tensor"),
            P("section", None, "tensor"),
            P("section", None, "tensor"),
            P("section", "tensor", None),
            P(),
            P(),
            P(),
            P(),
        ),
        out_specs=(P("section", None, "tensor", None), P("section", None, "tensor", None)),
        check_vma=False,
    )
```

```python
import functools

import jax
import jax.numpy as jnp
from jax import lax
from jax.experimental import pallas as pl
from jax.experimental.pallas import tpu as pltpu
from jax.sharding import PartitionSpec as P

HEAD_DIM = 128
RESP = 8

EPSILON = 1e-06
SOFT_CAP = 50.0
QUERY_SCALE = 1.0 / 12.0
LOSS_SCALE = 64.0

F32 = jnp.float32
BF16 = jnp.bfloat16
VMEM_LIMIT = 24 * 1024 * 1024
BATCH = 8


def shift(value, steps, sections=None):
    count = lax.axis_size("tensor")
    sections = range(lax.axis_size("section")) if sections is None else sections
    pairs = [(s * count + i, s * count + (i + steps) % count) for s in sections for i in range(count)]
    return lax.ppermute(value, ("section", "tensor"), pairs)


def swap_sections(value, first):
    count = lax.axis_size("section")
    pairs = []
    for s in range(first, count - 1, 2):
        pairs += [(s, s + 1), (s + 1, s)]
    return lax.ppermute(value, "section", pairs)


def dot(left, right):
    return lax.dot_general(left, right, (((1,), (0,)), ((), ())), preferred_element_type=F32)


def dot_nt(left, right):
    return lax.dot_general(left, right, (((1,), (1,)), ((), ())), preferred_element_type=F32)


def dot_tn(left, right):
    return lax.dot_general(left, right, (((0,), (0,)), ((), ())), preferred_element_type=F32)


def inv_rms(values):
    return lax.rsqrt(jnp.mean(values * values, axis=-1, keepdims=True) + EPSILON)


def pair_mask(block, length):
    row = lax.broadcasted_iota(jnp.int32, (block, block), 0)
    col = lax.broadcasted_iota(jnp.int32, (block, block), 1)
    return ((row // length == col // length) & (col <= row)).astype(F32)


def row_picks(positions, rows):
    return (positions == lax.broadcasted_iota(jnp.int32, (RESP, rows), 1)).astype(BF16)


def attention(queries, keys, mask):
    raw = [dot_nt(q, k) for q, k in zip(queries, keys)]
    capped = [jnp.tanh(r * (QUERY_SCALE / SOFT_CAP)) for r in raw]
    exps = [jnp.exp(SOFT_CAP * c) * mask for c in capped]
    sums = [jnp.sum(e, axis=-1, keepdims=True) for e in exps]
    return capped, [e / s for e, s in zip(exps, sums)]


def w_in_of(wq_ref, wk_ref, wv_ref):
    return jnp.concatenate([wq_ref[...], wk_ref[...], wv_ref[...]], axis=1)


def project(gain_ref, w_in, wo_ref, blocks):
    own = blocks[0].shape[0] // 2
    gain = gain_ref[...].astype(F32)
    normed = []
    for block in blocks:
        x_float = block[:own].astype(F32)
        normed.append((x_float * inv_rms(x_float) * gain).astype(BF16))
    normed = jnp.concatenate(normed, axis=0)
    cot = jnp.concatenate([block[own:] for block in blocks], axis=0)
    return dot(normed, w_in).astype(BF16), dot_nt(cot, wo_ref[...]).astype(BF16)


def early_kernel(gain_ref, wq_ref, wk_ref, wv_ref, wo_ref, *refs):
    blocks, out_ref = refs[:-1], refs[-1]
    w_in = w_in_of(wq_ref, wk_ref, wv_ref)
    own = blocks[0].shape[0] // 2
    for first in range(0, len(blocks), BATCH):
        some = blocks[first : first + BATCH]
        parts = project(gain_ref, w_in, wo_ref, some)
        rows = slice(first * own, (first + len(some)) * own)
        out_ref[rows, :] = jnp.concatenate(parts, axis=1)


def early_part(gain, weights, blocks):
    own, feats = blocks[0].shape[0] // 2, blocks[0].shape[1]
    rows, cols = own * len(blocks), sum(w.shape[1] for w in weights[:3]) + weights[3].shape[0]
    vmem = pl.BlockSpec(memory_space=pltpu.VMEM)
    return pl.pallas_call(
        early_kernel,
        out_shape=jax.ShapeDtypeStruct((rows, cols), BF16),
        in_specs=[vmem] * (5 + len(blocks)),
        out_specs=vmem,
        compiler_params=pltpu.CompilerParams(vmem_limit_bytes=VMEM_LIMIT),
        cost_estimate=pl.CostEstimate(
            flops=2 * rows * cols * feats, bytes_accessed=4 * rows * feats, transcendentals=0
        ),
        name="early_rows",
    )(gain, *weights, *blocks)


def place_all(offsets, me_ref, early_ref, late, qkv_ref, grad_ctx=None):
    count = len(offsets)
    cols = qkv_ref.shape[1]
    own = qkv_ref.shape[0] // count
    for i, offset in enumerate(offsets[:-1]):
        rows = pl.ds(place_of(me_ref, offset, count, own), own)
        qkv_ref[rows, :] = early_ref[i * own : (i + 1) * own, :cols]
        if grad_ctx is not None:
            grad_ctx[rows, :] = early_ref[i * own : (i + 1) * own, cols:]
    rows = pl.ds(place_of(me_ref, offsets[-1], count, own), own)
    qkv_ref[rows, :] = late[0]
    if grad_ctx is not None:
        grad_ctx[rows, :] = late[1]


def place_of(me_ref, offset, count, own):
    return pl.multiple_of(lax.rem(me_ref[0] + (offset + count), count) * own, own)


def pairs_of(qkv_ref, length, q_cols, kv_cols):
    block = 2 * length
    spans = [slice(start, start + block) for start in range(0, qkv_ref.shape[0], block)]
    pairs = [(s, h) for s in spans for h in range(0, q_cols, HEAD_DIM)]
    queries = [qkv_ref[s, h : h + HEAD_DIM] for s, h in pairs]
    keys = [qkv_ref[s, q_cols : q_cols + kv_cols] for s, h in pairs]
    values = [qkv_ref[s, q_cols + kv_cols :] for s, h in pairs]
    return spans, pairs, queries, keys, values


def rows_kernel(
    offsets,
    length,
    me_ref,
    positions_ref,
    gain_ref,
    wq_ref,
    wk_ref,
    wv_ref,
    wo_ref,
    early_ref,
    x_ref,
    late_ref,
    qkv_ref,
    rows_ref,
    context,
):
    own = qkv_ref.shape[0] // len(offsets)
    late = project(gain_ref, w_in_of(wq_ref, wk_ref, wv_ref), wo_ref, [late_ref])
    place_all(offsets, me_ref, early_ref, late, qkv_ref)
    q_cols, kv_cols = wq_ref.shape[1], wk_ref.shape[1]
    _, pairs, queries, keys, values = pairs_of(qkv_ref, length, q_cols, kv_cols)
    _, probs = attention(queries, keys, pair_mask(2 * length, length))
    for (s, h), prob, value in zip(pairs, probs, values):
        context[s, h : h + HEAD_DIM] = dot(prob.astype(BF16), value).astype(BF16)
    picks = row_picks(positions_ref[...], qkv_ref.shape[0])
    own_picks = row_picks(positions_ref[...] - me_ref[0] * own, own)
    rows_ref[...] = dot(dot(picks, context[...]).astype(BF16), wo_ref[...]) + dot(
        own_picks, x_ref[...]
    )


def rows_part_of(me, positions, gain, weights, early, x_own, late, offsets, length):
    own, feats = late.shape[0] // 2, late.shape[1]
    rows = own * len(offsets)
    vmem = pl.BlockSpec(memory_space=pltpu.VMEM)
    smem = pl.BlockSpec(memory_space=pltpu.SMEM)
    cols = sum(w.shape[1] for w in weights[:3])
    return pl.pallas_call(
        functools.partial(rows_kernel, offsets, length),
        out_shape=(
            jax.ShapeDtypeStruct((rows, cols), BF16),
            jax.ShapeDtypeStruct((RESP, feats), F32),
        ),
        in_specs=[smem] + [vmem] * 9,
        out_specs=[vmem] * 2,
        scratch_shapes=[pltpu.VMEM((rows, weights[0].shape[1]), BF16)],
        compiler_params=pltpu.CompilerParams(vmem_limit_bytes=VMEM_LIMIT),
        name="scored_rows",
    )(me, positions, gain, *weights, early, x_own, late)


def project_back(turned, wq_ref, wk_ref, wv_ref, wo_ref, mixed_outs, back_outs):
    own, feats = mixed_outs[0].shape[0], wq_ref.shape[0]
    at_mix = turned.shape[1] - wo_ref.shape[0]
    for start in range(0, feats, 256):
        cols = slice(start, start + 256)
        w_in = w_in_of(wq_ref.at[cols], wk_ref.at[cols], wv_ref.at[cols])
        back = dot_nt(turned[:, :at_mix], w_in).astype(BF16)
        mixed = dot(turned[:, at_mix:], wo_ref[:, cols]).astype(BF16)
        for j, (mixed_out, back_out) in enumerate(zip(mixed_outs, back_outs)):
            mixed_out[:, cols] = mixed[j * own : (j + 1) * own]
            back_out[:, cols] = back[j * own : (j + 1) * own]


def layer_kernel(
    offsets,
    back_offsets,
    length,
    me_ref,
    gain_ref,
    wq_ref,
    wk_ref,
    wv_ref,
    wo_ref,
    early_ref,
    late_ref,
    far_mixed_ref,
    far_back_ref,
    next_ref,
    rest_ref,
    qkv,
    grad_ctx,
    work,
    far_rows,
):
    count = len(offsets)
    own = late_ref.shape[0] // 2
    q_cols, kv_cols = wq_ref.shape[1], wk_ref.shape[1]
    late = project(gain_ref, w_in_of(wq_ref, wk_ref, wv_ref), wo_ref, [late_ref])
    place_all(offsets, me_ref, early_ref, late, qkv, grad_ctx)
    spans, pairs, queries, keys, values = pairs_of(qkv, length, q_cols, kv_cols)
    ctxs = [grad_ctx[s, h : h + HEAD_DIM] for s, h in pairs]
    capped, probs = attention(queries, keys, pair_mask(2 * length, length))
    grad_probs = [dot_nt(c, v) for c, v in zip(ctxs, values)]
    means = [jnp.sum(p * g, axis=-1, keepdims=True) for p, g in zip(probs, grad_probs)]
    raws = [
        (p * (g - m) * (1.0 - c * c) * QUERY_SCALE).astype(BF16)
        for p, g, m, c in zip(probs, grad_probs, means, capped)
    ]
    probs = [p.astype(BF16) for p in probs]
    mixes = [dot(p, v).astype(BF16) for p, v in zip(probs, values)]
    grad_queries = [dot(r, k).astype(BF16) for r, k in zip(raws, keys)]
    grad_keys = [dot_tn(r, q) for r, q in zip(raws, queries)]
    grad_values = [dot_tn(p, c) for p, c in zip(probs, ctxs)]
    per = q_cols // HEAD_DIM
    at_keys, at_values, at_mix = q_cols, q_cols + kv_cols, q_cols + 2 * kv_cols
    for (s, h), grad_query, mix in zip(pairs, grad_queries, mixes):
        work[s, h : h + HEAD_DIM] = grad_query
        work[s, at_mix + h : at_mix + h + HEAD_DIM] = mix
    for i, s in enumerate(spans):
        work[s, at_keys:at_values] = sum(grad_keys[i * per : (i + 1) * per]).astype(BF16)
        work[s, at_values:at_mix] = sum(grad_values[i * per : (i + 1) * per]).astype(BF16)
    for i, offset in enumerate(back_offsets):
        rows = work[pl.ds(place_of(me_ref, offset, count, own), own), :]
        if i == 0:
            far_rows[...] = rows
        elif i <= 2:
            next_ref[(i - 1) * own : i * own, :] = rows
        else:
            rest_ref[(i - 3) * own : (i - 2) * own, :] = rows
    project_back(far_rows, wq_ref, wk_ref, wv_ref, wo_ref, [far_mixed_ref], [far_back_ref])


def rest_kernel(wq_ref, wk_ref, wv_ref, wo_ref, rest_ref, *outs):
    own = outs[0].shape[0] // 2
    mixed_outs = [out.at[:own] for out in outs]
    back_outs = [out.at[own:] for out in outs]
    project_back(rest_ref, wq_ref, wk_ref, wv_ref, wo_ref, mixed_outs, back_outs)


def layer_part(me, gain, weights, early, late, offsets, back_offsets, length):
    count = len(offsets)
    own, feats = late.shape[0] // 2, late.shape[1]
    rows = own * count
    vmem = pl.BlockSpec(memory_space=pltpu.VMEM)
    smem = pl.BlockSpec(memory_space=pltpu.SMEM)
    cols, q_cols = sum(w.shape[1] for w in weights[:3]), weights[0].shape[1]
    far_term = jax.ShapeDtypeStruct((own, feats), BF16)
    return pl.pallas_call(
        functools.partial(layer_kernel, offsets, back_offsets, length),
        out_shape=(
            far_term,
            far_term,
            jax.ShapeDtypeStruct((2 * own, cols + q_cols), BF16),
            jax.ShapeDtypeStruct((rows - 3 * own, cols + q_cols), BF16),
        ),
        in_specs=[smem] + [vmem] * 7,
        out_specs=[vmem] * 4,
        scratch_shapes=[
            pltpu.VMEM((rows, cols), BF16),
            pltpu.VMEM((rows, q_cols), BF16),
            pltpu.VMEM((rows, cols + q_cols), BF16),
            pltpu.VMEM((own, cols + q_cols), BF16),
        ],
        compiler_params=pltpu.CompilerParams(vmem_limit_bytes=VMEM_LIMIT),
        name="layer_both_ways",
    )(me, gain, *weights, early, late)


def terms_of(weights, turned, own):
    count, feats = turned.shape[0] // own, weights[0].shape[0]
    vmem = pl.BlockSpec(memory_space=pltpu.VMEM)
    return pl.pallas_call(
        rest_kernel,
        out_shape=[jax.ShapeDtypeStruct((2 * own, feats), BF16)] * count,
        in_specs=[vmem] * 5,
        out_specs=[vmem] * count,
        compiler_params=pltpu.CompilerParams(vmem_limit_bytes=VMEM_LIMIT),
        cost_estimate=pl.CostEstimate(
            flops=2 * turned.size * feats, bytes_accessed=0, transcendentals=0
        ),
        name="rest_of_terms",
    )(*weights, turned)


def scored_kernel(
    count,
    length,
    positions_ref,
    row_grads_ref,
    qkv_ref,
    wq_ref,
    wk_ref,
    wv_ref,
    wo_ref,
    parcels_ref,
):
    rows = qkv_ref.shape[0]
    feats = wq_ref.shape[0]
    own = rows // count
    q_cols, kv_cols = wq_ref.shape[1], wk_ref.shape[1]
    positions = positions_ref[...]
    picks = row_picks(positions, rows)
    row = lax.broadcasted_iota(jnp.int32, (RESP, rows), 0)
    col = lax.broadcasted_iota(jnp.int32, (RESP, rows), 1)
    mask = ((col // length == row) & (col <= positions)).astype(F32)
    query_all = dot(picks, qkv_ref[:, :q_cols]).astype(BF16)
    ctx_all = dot_nt(row_grads_ref[...].astype(BF16), wo_ref[...]).astype(BF16)
    keys = qkv_ref[:, q_cols : q_cols + kv_cols]
    values = qkv_ref[:, q_cols + kv_cols :]
    heads = range(0, q_cols, HEAD_DIM)
    queries = [query_all[:, h : h + HEAD_DIM] for h in heads]
    ctxs = [ctx_all[:, h : h + HEAD_DIM] for h in heads]
    capped, probs = attention(queries, [keys] * len(heads), mask)
    raws = []
    for prob, cap, ctx in zip(probs, capped, ctxs):
        grad_prob = dot_nt(ctx, values)
        grad_score = prob * (grad_prob - jnp.sum(prob * grad_prob, axis=-1, keepdims=True))
        raws.append((grad_score * (1.0 - cap * cap) * QUERY_SCALE).astype(BF16))
    grad_query = jnp.concatenate([dot(raw, keys) for raw in raws], axis=1).astype(BF16)
    vectors = [dot_nt(q, wk_ref[...]) for q in queries] + [dot_nt(c, wv_ref[...]) for c in ctxs]
    vectors.append(dot_nt(grad_query, wq_ref[...]))
    fold_row = lax.broadcasted_iota(jnp.int32, (rows, length), 0)
    fold_col = lax.broadcasted_iota(jnp.int32, (rows, length), 1)
    fold = (fold_row % length == fold_col).astype(BF16)
    shares = [dot(c, fold) for c in raws + [p.astype(BF16) for p in probs] + [picks]]
    kinds = len(vectors)
    vectors = jnp.concatenate(vectors, axis=0).astype(BF16)
    shares = jnp.concatenate(shares, axis=0).astype(BF16)
    slots = parcels_ref.shape[0] // count
    out_row = lax.broadcasted_iota(jnp.int32, (count * slots, kinds * RESP), 0)
    source = lax.broadcasted_iota(jnp.int32, (count * slots, kinds * RESP), 1)
    owner, slot = out_row // slots, out_row % slots
    choose = ((slot == source // RESP) & (owner // (length // own) == source % RESP)).astype(BF16)
    share = length // own
    half = (lax.broadcasted_iota(jnp.int32, (count * slots, 1), 0) // slots) % share
    width = feats // share
    lanes = jnp.zeros((count * slots, width), F32)
    chosen = dot(choose, shares)
    part = jnp.zeros((count * slots, own), F32)
    for i in range(share):
        lanes = jnp.where(half == i, dot(choose, vectors[:, i * width : (i + 1) * width]), lanes)
        part = jnp.where(half == i, chosen[:, i * own : (i + 1) * own], part)
    parcels_ref[:, :width] = lanes.astype(BF16)
    tail = jnp.zeros((count * slots, 128 - own), F32)
    parcels_ref[:, width:] = jnp.concatenate([part, tail], axis=1).astype(BF16)


def scored_part(positions, row_grads, qkv, weights, count, length, section):
    width = row_grads.shape[1] // 2
    own = qkv.shape[0] // count
    vmem = pl.BlockSpec(memory_space=pltpu.VMEM)
    slots = 8
    parcels = pl.pallas_call(
        functools.partial(scored_kernel, count, length),
        out_shape=jax.ShapeDtypeStruct((count * slots, width + 128), BF16),
        in_specs=[vmem] * 7,
        out_specs=vmem,
        compiler_params=pltpu.CompilerParams(vmem_limit_bytes=VMEM_LIMIT),
        name="scored_backward",
    )(positions, row_grads, qkv, *weights)
    parcels = lax.all_to_all(parcels.reshape(count, slots, -1), "tensor", 0, 0)
    parcels = parcels.reshape(count * slots, -1)
    vectors, shares = parcels[:, :width], parcels[:, width : width + own]
    swaps = [(section * count + i, section * count + (i ^ 1)) for i in range(count)]
    swapped = lax.ppermute(vectors, ("section", "tensor"), swaps)
    mine, theirs = dot_tn(shares, vectors), dot_tn(shares, swapped)
    second = lax.axis_index("tensor") % 2 == 1
    return jnp.concatenate(
        [jnp.where(second, theirs, mine), jnp.where(second, mine, theirs)], axis=1
    )


def finish_kernel(
    me_ref, positions_ref, gain_ref, x_ref, later_ref, sums_ref, row_grads_ref, between_ref, within_ref
):
    own = x_ref.shape[0]
    x = x_ref[...].astype(F32)
    hidden = x + sums_ref[:own]
    picks = row_picks(positions_ref[...] - me_ref[0] * own, own)
    last = dot_tn(picks, row_grads_ref[...].astype(BF16))
    cotangent = jnp.where(me_ref[2] == 1, last, later_ref[...].astype(F32))
    inv_x = inv_rms(x)
    scaled = sums_ref[own:] * gain_ref[...].astype(F32)
    mean = jnp.mean(scaled * x, axis=-1, keepdims=True)
    returned = cotangent + inv_x * scaled - x * (inv_x * inv_x * inv_x * mean)
    odd = me_ref[1] == 1
    between_ref[...] = jnp.where(odd, hidden, returned).astype(BF16)
    within_ref[...] = jnp.where(odd, returned, hidden).astype(BF16)


def finish_part(me, positions, gain, x_own, later_own, sums, row_grads):
    vmem = pl.BlockSpec(memory_space=pltpu.VMEM)
    smem = pl.BlockSpec(memory_space=pltpu.SMEM)
    return pl.pallas_call(
        finish_kernel,
        out_shape=[jax.ShapeDtypeStruct(x_own.shape, BF16)] * 2,
        in_specs=[smem] + [vmem] * 6,
        out_specs=[vmem] * 2,
        compiler_params=pltpu.CompilerParams(vmem_limit_bytes=VMEM_LIMIT),
        name="finish",
    )(me, positions, gain, x_own, later_own, sums, row_grads)


def rank_grad(reward_scores, rankings):
    slots = jnp.arange(RESP)
    order_hot = (rankings[0][:, None] == slots[None, :]).astype(F32)
    ordered = jnp.sum(order_hot * reward_scores[None, :], axis=1)
    exp_order = jnp.exp(ordered)
    upper = (slots[:, None] >= slots[None, :]).astype(F32)
    suffix = jnp.sum(exp_order[:, None] * upper, axis=0)
    cumulative = jnp.sum((1.0 / suffix)[None, :] * upper, axis=1)
    grad_order = LOSS_SCALE * (exp_order * cumulative - 1.0)
    return jnp.sum(order_hot * grad_order[:, None], axis=0)


def gather_ring(block):
    count = lax.axis_size("tensor")
    blocks, offsets = [block], [0]
    up = down = block
    for step in range(1, count // 2 + 1):
        up = shift(up, 1)
        blocks.append(up)
        offsets.append(-step)
        if step < count - count // 2:
            down = shift(down, -1)
            blocks.append(down)
            offsets.append(step)
    return blocks, offsets


def scatter_ring(weights, far_mixed, far_back, next_rows, rest_rows, back_offsets, sections):
    far = lax.axis_size("tensor") // 2
    own = far_mixed.shape[0]
    none = jnp.zeros(far_mixed.shape, F32)
    up, down = shift(far_mixed, 1, sections), shift(far_back, -1, sections)
    terms = dict(zip(back_offsets[1:3], terms_of(weights, next_rows, own)))
    up = jnp.concatenate([up.astype(F32), none])
    down = jnp.concatenate([none, down.astype(F32)])
    for left in range(far - 1, 0, -1):
        up = (up.astype(F32) + terms[left].astype(F32)).astype(BF16)
        down = (down.astype(F32) + terms[-left].astype(F32)).astype(BF16)
        if left == far - 1:
            up, down, rest_rows = lax.optimization_barrier((up, down, rest_rows))
            terms.update(zip(back_offsets[3:], terms_of(weights, rest_rows, own)))
        up, down = shift(up, 1, sections), shift(down, -1, sections)
    return terms[0].astype(F32) + up.astype(F32) + down.astype(F32)


def sum_rows(value, sections):
    step = 1
    while step < lax.axis_size("tensor"):
        value = value + shift(value, step, sections)
        step *= 2
    return value


def shards(
    section_inputs,
    later_grad,
    attn_gain,
    w_query,
    w_key,
    w_value,
    w_out,
    final_gain,
    reward_head,
    rankings,
    lengths,
):
    x_own = section_inputs[0, 0]
    later_own = later_grad[0, 0]
    own_count = x_own.shape[0]
    tensor_count = lax.axis_size("tensor")
    tensor_pos = lax.axis_index("tensor")
    total_rows = own_count * tensor_count
    length = total_rows // RESP
    weights = (w_query[0], w_key[0], w_value[0], w_out[0])
    at_end = lax.axis_index("section") == lax.axis_size("section") - 1
    positions = jnp.arange(RESP) * length + lengths[0] - 1
    places = positions[:, None].astype(jnp.int32)
    odd = lax.axis_index("section") % 2
    me = jnp.stack([tensor_pos, odd, at_end]).astype(jnp.int32)

    last = lax.axis_size("section") - 1
    blocks, offsets = gather_ring(jnp.concatenate([x_own, later_own]))
    far = tensor_count // 2
    back_offsets = [far, far - 1, 1 - far, *range(2 - far, far - 1)]
    early = early_part(attn_gain, weights, blocks[:-1])

    def inner_section(early, late):
        parts = layer_part(me, attn_gain, weights, early, late, offsets, back_offsets, length)
        sums = scatter_ring(weights, *parts, back_offsets, range(last))
        return sums, jnp.zeros((RESP, x_own.shape[1]), F32)

    def last_section(early, late):
        qkv, rows_part = rows_part_of(
            me, places, attn_gain, weights, early, x_own, late, offsets, length
        )
        rows_hidden = sum_rows(rows_part, [last]).astype(BF16).astype(F32)
        inv_norm = inv_rms(rows_hidden)
        head_vec = final_gain.astype(F32) * reward_head.astype(F32)
        reward_scores = jnp.sum(rows_hidden * inv_norm * head_vec, axis=-1)
        scaled = rank_grad(reward_scores, rankings)[:, None] * head_vec
        row_grads = inv_norm * scaled - rows_hidden * inv_norm**3 * jnp.mean(
            scaled * rows_hidden, axis=-1, keepdims=True
        )
        row_grads = row_grads.astype(BF16).astype(F32)
        back_own = scored_part(
            places, row_grads, qkv, weights, tensor_count, length, last
        )
        return jnp.concatenate([jnp.zeros_like(back_own), back_own]), row_grads

    sums, row_grads = lax.cond(at_end, last_section, inner_section, early, blocks[-1])
    between, within = finish_part(me, places, attn_gain, x_own, later_own, sums, row_grads)
    between, within = swap_sections(between, 1), swap_sections(within, 0)
    even = lax.axis_index("section") % 2 == 0
    arrived = jnp.where(even, between, within)
    sent_back = jnp.where(even, within, between)
    return (arrived[None, None], sent_back[None, None])


def solution(mesh):
    return jax.shard_map(
        shards,
        mesh=mesh,
        in_specs=(
            P("section", None, "tensor", None),
            P("section", None, "tensor", None),
            P("section", None),
            P("section", None, "tensor"),
            P("section", None, "tensor"),
            P("section", None, "tensor"),
            P("section", "tensor", None),
            P(),
            P(),
            P(),
            P(),
        ),
        out_specs=(P("section", None, "tensor", None), P("section", None, "tensor", None)),
        check_vma=False,
    )
```

```python
import functools

import jax
import jax.numpy as jnp
from jax import lax
from jax.experimental import pallas as pl
from jax.experimental.pallas import tpu as pltpu
from jax.sharding import PartitionSpec as P

HEAD_DIM = 128
RESP = 8

EPSILON = 1e-06
SOFT_CAP = 50.0
QUERY_SCALE = 1.0 / 12.0
LOSS_SCALE = 64.0

F32 = jnp.float32
BF16 = jnp.bfloat16
VMEM_LIMIT = 24 * 1024 * 1024
BATCH = 8


def shift(value, steps, sections=None):
    count = lax.axis_size("tensor")
    sections = range(lax.axis_size("section")) if sections is None else sections
    pairs = [(s * count + i, s * count + (i + steps) % count) for s in sections for i in range(count)]
    return lax.ppermute(value, ("section", "tensor"), pairs)


def swap_sections(value, first):
    count = lax.axis_size("section")
    pairs = []
    for s in range(first, count - 1, 2):
        pairs += [(s, s + 1), (s + 1, s)]
    return lax.ppermute(value, "section", pairs)


def dot(left, right):
    return lax.dot_general(left, right, (((1,), (0,)), ((), ())), preferred_element_type=F32)


def dot_nt(left, right):
    return lax.dot_general(left, right, (((1,), (1,)), ((), ())), preferred_element_type=F32)


def dot_tn(left, right):
    return lax.dot_general(left, right, (((0,), (0,)), ((), ())), preferred_element_type=F32)


def inv_rms(values):
    return lax.rsqrt(jnp.mean(values * values, axis=-1, keepdims=True) + EPSILON)


def pair_mask(block, length):
    row = lax.broadcasted_iota(jnp.int32, (block, block), 0)
    col = lax.broadcasted_iota(jnp.int32, (block, block), 1)
    return ((row // length == col // length) & (col <= row)).astype(F32)


def row_picks(positions, rows):
    return (positions == lax.broadcasted_iota(jnp.int32, (RESP, rows), 1)).astype(BF16)


def attention(queries, keys, mask):
    raw = [dot_nt(q, k) for q, k in zip(queries, keys)]
    capped = [jnp.tanh(r * (QUERY_SCALE / SOFT_CAP)) for r in raw]
    exps = [jnp.exp(SOFT_CAP * c) * mask for c in capped]
    sums = [jnp.sum(e, axis=-1, keepdims=True) for e in exps]
    return capped, [e / s for e, s in zip(exps, sums)]


def w_in_of(wq_ref, wk_ref, wv_ref):
    return jnp.concatenate([wq_ref[...], wk_ref[...], wv_ref[...]], axis=1)


def project(gain_ref, w_in, wo_ref, blocks):
    own = blocks[0].shape[0] // 2
    gain = gain_ref[...].astype(F32)
    normed = []
    for block in blocks:
        x_float = block[:own].astype(F32)
        normed.append((x_float * inv_rms(x_float) * gain).astype(BF16))
    normed = jnp.concatenate(normed, axis=0)
    cot = jnp.concatenate([block[own:] for block in blocks], axis=0)
    return dot(normed, w_in).astype(BF16), dot_nt(cot, wo_ref[...]).astype(BF16)


def early_kernel(gain_ref, wq_ref, wk_ref, wv_ref, wo_ref, *refs):
    blocks, out_ref = refs[:-1], refs[-1]
    w_in = w_in_of(wq_ref, wk_ref, wv_ref)
    own = blocks[0].shape[0] // 2
    for first in range(0, len(blocks), BATCH):
        some = blocks[first : first + BATCH]
        parts = project(gain_ref, w_in, wo_ref, some)
        rows = slice(first * own, (first + len(some)) * own)
        out_ref[rows, :] = jnp.concatenate(parts, axis=1)


def early_part(gain, weights, blocks):
    own, feats = blocks[0].shape[0] // 2, blocks[0].shape[1]
    rows, cols = own * len(blocks), sum(w.shape[1] for w in weights[:3]) + weights[3].shape[0]
    vmem = pl.BlockSpec(memory_space=pltpu.VMEM)
    return pl.pallas_call(
        early_kernel,
        out_shape=jax.ShapeDtypeStruct((rows, cols), BF16),
        in_specs=[vmem] * (5 + len(blocks)),
        out_specs=vmem,
        compiler_params=pltpu.CompilerParams(vmem_limit_bytes=VMEM_LIMIT),
        cost_estimate=pl.CostEstimate(
            flops=2 * rows * cols * feats, bytes_accessed=4 * rows * feats, transcendentals=0
        ),
        name="early_rows",
    )(gain, *weights, *blocks)


def place_all(offsets, me_ref, early_ref, late, qkv_ref, grad_ctx=None):
    count = len(offsets)
    cols = qkv_ref.shape[1]
    own = qkv_ref.shape[0] // count
    for i, offset in enumerate(offsets[:-1]):
        rows = pl.ds(place_of(me_ref, offset, count, own), own)
        qkv_ref[rows, :] = early_ref[i * own : (i + 1) * own, :cols]
        if grad_ctx is not None:
            grad_ctx[rows, :] = early_ref[i * own : (i + 1) * own, cols:]
    rows = pl.ds(place_of(me_ref, offsets[-1], count, own), own)
    qkv_ref[rows, :] = late[0]
    if grad_ctx is not None:
        grad_ctx[rows, :] = late[1]


def place_of(me_ref, offset, count, own):
    return pl.multiple_of(lax.rem(me_ref[0] + (offset + count), count) * own, own)


def pairs_of(qkv_ref, length, q_cols, kv_cols):
    block = 2 * length
    spans = [slice(start, start + block) for start in range(0, qkv_ref.shape[0], block)]
    pairs = [(s, h) for s in spans for h in range(0, q_cols, HEAD_DIM)]
    queries = [qkv_ref[s, h : h + HEAD_DIM] for s, h in pairs]
    keys = [qkv_ref[s, q_cols : q_cols + kv_cols] for s, h in pairs]
    values = [qkv_ref[s, q_cols + kv_cols :] for s, h in pairs]
    return spans, pairs, queries, keys, values


def rows_kernel(
    offsets,
    length,
    me_ref,
    positions_ref,
    gain_ref,
    wq_ref,
    wk_ref,
    wv_ref,
    wo_ref,
    early_ref,
    x_ref,
    late_ref,
    qkv_ref,
    rows_ref,
    context,
):
    own = qkv_ref.shape[0] // len(offsets)
    late = project(gain_ref, w_in_of(wq_ref, wk_ref, wv_ref), wo_ref, [late_ref])
    place_all(offsets, me_ref, early_ref, late, qkv_ref)
    q_cols, kv_cols = wq_ref.shape[1], wk_ref.shape[1]
    _, pairs, queries, keys, values = pairs_of(qkv_ref, length, q_cols, kv_cols)
    _, probs = attention(queries, keys, pair_mask(2 * length, length))
    for (s, h), prob, value in zip(pairs, probs, values):
        context[s, h : h + HEAD_DIM] = dot(prob.astype(BF16), value).astype(BF16)
    picks = row_picks(positions_ref[...], qkv_ref.shape[0])
    own_picks = row_picks(positions_ref[...] - me_ref[0] * own, own)
    rows_ref[...] = dot(dot(picks, context[...]).astype(BF16), wo_ref[...]) + dot(
        own_picks, x_ref[...]
    )


def rows_part_of(me, positions, gain, weights, early, x_own, late, offsets, length):
    own, feats = late.shape[0] // 2, late.shape[1]
    rows = own * len(offsets)
    vmem = pl.BlockSpec(memory_space=pltpu.VMEM)
    smem = pl.BlockSpec(memory_space=pltpu.SMEM)
    cols = sum(w.shape[1] for w in weights[:3])
    return pl.pallas_call(
        functools.partial(rows_kernel, offsets, length),
        out_shape=(
            jax.ShapeDtypeStruct((rows, cols), BF16),
            jax.ShapeDtypeStruct((RESP, feats), F32),
        ),
        in_specs=[smem] + [vmem] * 9,
        out_specs=[vmem] * 2,
        scratch_shapes=[pltpu.VMEM((rows, weights[0].shape[1]), BF16)],
        compiler_params=pltpu.CompilerParams(vmem_limit_bytes=VMEM_LIMIT),
        name="scored_rows",
    )(me, positions, gain, *weights, early, x_own, late)


def project_back(turned, wq_ref, wk_ref, wv_ref, wo_ref, mixed_outs, back_outs):
    own, feats = mixed_outs[0].shape[0], wq_ref.shape[0]
    at_mix = turned.shape[1] - wo_ref.shape[0]
    for start in range(0, feats, 256):
        cols = slice(start, start + 256)
        w_in = w_in_of(wq_ref.at[cols], wk_ref.at[cols], wv_ref.at[cols])
        back = dot_nt(turned[:, :at_mix], w_in).astype(BF16)
        mixed = dot(turned[:, at_mix:], wo_ref[:, cols]).astype(BF16)
        for j, (mixed_out, back_out) in enumerate(zip(mixed_outs, back_outs)):
            mixed_out[:, cols] = mixed[j * own : (j + 1) * own]
            back_out[:, cols] = back[j * own : (j + 1) * own]


def layer_kernel(
    offsets,
    back_offsets,
    length,
    me_ref,
    gain_ref,
    wq_ref,
    wk_ref,
    wv_ref,
    wo_ref,
    early_ref,
    late_ref,
    far_mixed_ref,
    far_back_ref,
    next_ref,
    rest_ref,
    qkv,
    grad_ctx,
    work,
    far_rows,
):
    count = len(offsets)
    own = late_ref.shape[0] // 2
    q_cols, kv_cols = wq_ref.shape[1], wk_ref.shape[1]
    late = project(gain_ref, w_in_of(wq_ref, wk_ref, wv_ref), wo_ref, [late_ref])
    place_all(offsets, me_ref, early_ref, late, qkv, grad_ctx)
    spans, pairs, queries, keys, values = pairs_of(qkv, length, q_cols, kv_cols)
    ctxs = [grad_ctx[s, h : h + HEAD_DIM] for s, h in pairs]
    capped, probs = attention(queries, keys, pair_mask(2 * length, length))
    grad_probs = [dot_nt(c, v) for c, v in zip(ctxs, values)]
    means = [jnp.sum(p * g, axis=-1, keepdims=True) for p, g in zip(probs, grad_probs)]
    raws = [
        (p * (g - m) * (1.0 - c * c) * QUERY_SCALE).astype(BF16)
        for p, g, m, c in zip(probs, grad_probs, means, capped)
    ]
    probs = [p.astype(BF16) for p in probs]
    mixes = [dot(p, v).astype(BF16) for p, v in zip(probs, values)]
    grad_queries = [dot(r, k).astype(BF16) for r, k in zip(raws, keys)]
    grad_keys = [dot_tn(r, q) for r, q in zip(raws, queries)]
    grad_values = [dot_tn(p, c) for p, c in zip(probs, ctxs)]
    per = q_cols // HEAD_DIM
    at_keys, at_values, at_mix = q_cols, q_cols + kv_cols, q_cols + 2 * kv_cols
    for (s, h), grad_query, mix in zip(pairs, grad_queries, mixes):
        work[s, h : h + HEAD_DIM] = grad_query
        work[s, at_mix + h : at_mix + h + HEAD_DIM] = mix
    for i, s in enumerate(spans):
        work[s, at_keys:at_values] = sum(grad_keys[i * per : (i + 1) * per]).astype(BF16)
        work[s, at_values:at_mix] = sum(grad_values[i * per : (i + 1) * per]).astype(BF16)
    for i, offset in enumerate(back_offsets):
        rows = work[pl.ds(place_of(me_ref, offset, count, own), own), :]
        if i == 0:
            far_rows[...] = rows
        elif i <= 2:
            next_ref[(i - 1) * own : i * own, :] = rows
        else:
            rest_ref[(i - 3) * own : (i - 2) * own, :] = rows
    project_back(far_rows, wq_ref, wk_ref, wv_ref, wo_ref, [far_mixed_ref], [far_back_ref])


def rest_kernel(wq_ref, wk_ref, wv_ref, wo_ref, rest_ref, *outs):
    own = outs[0].shape[0] // 2
    mixed_outs = [out.at[:own] for out in outs]
    back_outs = [out.at[own:] for out in outs]
    project_back(rest_ref, wq_ref, wk_ref, wv_ref, wo_ref, mixed_outs, back_outs)


def layer_part(me, gain, weights, early, late, offsets, back_offsets, length):
    count = len(offsets)
    own, feats = late.shape[0] // 2, late.shape[1]
    rows = own * count
    vmem = pl.BlockSpec(memory_space=pltpu.VMEM)
    smem = pl.BlockSpec(memory_space=pltpu.SMEM)
    cols, q_cols = sum(w.shape[1] for w in weights[:3]), weights[0].shape[1]
    far_term = jax.ShapeDtypeStruct((own, feats), BF16)
    return pl.pallas_call(
        functools.partial(layer_kernel, offsets, back_offsets, length),
        out_shape=(
            far_term,
            far_term,
            jax.ShapeDtypeStruct((2 * own, cols + q_cols), BF16),
            jax.ShapeDtypeStruct((rows - 3 * own, cols + q_cols), BF16),
        ),
        in_specs=[smem] + [vmem] * 7,
        out_specs=[vmem] * 4,
        scratch_shapes=[
            pltpu.VMEM((rows, cols), BF16),
            pltpu.VMEM((rows, q_cols), BF16),
            pltpu.VMEM((rows, cols + q_cols), BF16),
            pltpu.VMEM((own, cols + q_cols), BF16),
        ],
        compiler_params=pltpu.CompilerParams(vmem_limit_bytes=VMEM_LIMIT),
        name="layer_both_ways",
    )(me, gain, *weights, early, late)


def terms_of(weights, turned, own):
    count, feats = turned.shape[0] // own, weights[0].shape[0]
    vmem = pl.BlockSpec(memory_space=pltpu.VMEM)
    return pl.pallas_call(
        rest_kernel,
        out_shape=[jax.ShapeDtypeStruct((2 * own, feats), BF16)] * count,
        in_specs=[vmem] * 5,
        out_specs=[vmem] * count,
        compiler_params=pltpu.CompilerParams(vmem_limit_bytes=VMEM_LIMIT),
        cost_estimate=pl.CostEstimate(
            flops=2 * turned.size * feats, bytes_accessed=0, transcendentals=0
        ),
        name="rest_of_terms",
    )(*weights, turned)


def scored_kernel(
    count,
    length,
    positions_ref,
    row_grads_ref,
    qkv_ref,
    wq_ref,
    wk_ref,
    wv_ref,
    wo_ref,
    parcels_ref,
    packed,
):
    rows = qkv_ref.shape[0]
    feats = wq_ref.shape[0]
    own = rows // count
    q_cols, kv_cols = wq_ref.shape[1], wk_ref.shape[1]
    positions = positions_ref[...]
    picks = row_picks(positions, rows)
    row = lax.broadcasted_iota(jnp.int32, (RESP, rows), 0)
    col = lax.broadcasted_iota(jnp.int32, (RESP, rows), 1)
    mask = ((col // length == row) & (col <= positions)).astype(F32)
    query_all = dot(picks, qkv_ref[:, :q_cols]).astype(BF16)
    ctx_all = dot_nt(row_grads_ref[...].astype(BF16), wo_ref[...]).astype(BF16)
    keys = qkv_ref[:, q_cols : q_cols + kv_cols]
    values = qkv_ref[:, q_cols + kv_cols :]
    heads = range(0, q_cols, HEAD_DIM)
    queries = [query_all[:, h : h + HEAD_DIM] for h in heads]
    ctxs = [ctx_all[:, h : h + HEAD_DIM] for h in heads]
    capped, probs = attention(queries, [keys] * len(heads), mask)
    raws = []
    for prob, cap, ctx in zip(probs, capped, ctxs):
        grad_prob = dot_nt(ctx, values)
        grad_score = prob * (grad_prob - jnp.sum(prob * grad_prob, axis=-1, keepdims=True))
        raws.append((grad_score * (1.0 - cap * cap) * QUERY_SCALE).astype(BF16))
    grad_query = jnp.concatenate([dot(raw, keys) for raw in raws], axis=1).astype(BF16)
    vectors = [dot_nt(q, wk_ref[...]) for q in queries] + [dot_nt(c, wv_ref[...]) for c in ctxs]
    vectors.append(dot_nt(grad_query, wq_ref[...]))
    fold_row = lax.broadcasted_iota(jnp.int32, (rows, length), 0)
    fold_col = lax.broadcasted_iota(jnp.int32, (rows, length), 1)
    fold = (fold_row % length == fold_col).astype(BF16)
    shares = [dot(c, fold) for c in raws + [p.astype(BF16) for p in probs] + [picks]]
    owners = length // own
    lanes, slots, width, half = parcel_shape(len(vectors), feats, owners)
    stride = owners * slots
    packed[...] = jnp.zeros(packed.shape, F32)
    for i in range(len(vectors) * feats // lanes):
        vector, place = divmod(i * lanes, feats)
        owner, block = divmod(i, half)
        slot, at = divmod(block * lanes, width)
        packed[at // lanes, pl.ds(owner * slots + slot, RESP, stride=stride), :] = vectors[vector][
            :, place : place + lanes
        ]
    per = lanes // own
    for owner in range(owners):
        for first in range(0, len(shares), per):
            slot, at = divmod((half + first // per) * lanes, width)
            some = [s[:, owner * own : (owner + 1) * own] for s in shares[first : first + per]]
            some += [jnp.zeros((RESP, own), F32)] * (per - len(some))
            packed[at // lanes, pl.ds(owner * slots + slot, RESP, stride=stride), :] = (
                jnp.concatenate(some, axis=1)
            )
    for i in range(width // lanes):
        parcels_ref[:, i * lanes : (i + 1) * lanes] = packed[i].astype(BF16)


def parcel_shape(kinds, feats, owners):
    lanes, slots = 128, 8
    half = kinds * feats // lanes // owners
    blocks = half + 2
    return lanes, slots, -(-blocks // slots) * lanes, half


def unpack_kernel(kinds, me_ref, mine_ref, theirs_ref, out_ref, mine, theirs):
    own, feats = out_ref.shape
    owners = 2
    lanes, slots, width, half = parcel_shape(kinds, feats, owners)
    count = mine_ref.shape[0] // slots
    for i in range(width // lanes):
        mine[i] = mine_ref[:, i * lanes : (i + 1) * lanes].astype(F32)
        theirs[i] = theirs_ref[:, i * lanes : (i + 1) * lanes].astype(F32)
    second = lax.rem(me_ref[0], owners) == 1

    def block_of(ref, block):
        slot, at = divmod(block * lanes, width)
        return ref[at // lanes, pl.ds(slot, count, stride=slots), :]

    per = lanes // own
    shares = [block_of(mine, half + k // per)[:, k % per * own : (k % per + 1) * own] for k in range(kinds)]
    shares = jnp.concatenate(shares, axis=0).astype(BF16)
    for place in range(0, feats, lanes):
        parts = []
        for vector in range(kinds):
            owner, block = divmod((vector * feats + place) // lanes, half)
            here, there = block_of(mine, block), block_of(theirs, block)
            swap = second if owner == 0 else jnp.logical_not(second)
            parts.append(jnp.where(swap, there, here))
        out_ref[:, place : place + lanes] = dot_tn(shares, jnp.concatenate(parts, axis=0).astype(BF16))


def scored_part(me, positions, row_grads, qkv, weights, count, length, section):
    feats = row_grads.shape[1]
    own = qkv.shape[0] // count
    vmem = pl.BlockSpec(memory_space=pltpu.VMEM)
    smem = pl.BlockSpec(memory_space=pltpu.SMEM)
    kinds = 2 * (weights[0].shape[1] // HEAD_DIM) + 1
    lanes, slots, width, _ = parcel_shape(kinds, feats, length // own)
    shape = (count * slots, width)
    blocks = pltpu.VMEM((width // lanes, count * slots, lanes), F32)
    parcels = pl.pallas_call(
        functools.partial(scored_kernel, count, length),
        out_shape=jax.ShapeDtypeStruct(shape, BF16),
        in_specs=[vmem] * 7,
        out_specs=vmem,
        scratch_shapes=[blocks],
        compiler_params=pltpu.CompilerParams(vmem_limit_bytes=VMEM_LIMIT),
        name="scored_backward",
    )(positions, row_grads, qkv, *weights)
    mine = lax.all_to_all(parcels.reshape(count, slots, width), "tensor", 0, 0).reshape(shape)
    swaps = [(section * count + i, section * count + (i ^ 1)) for i in range(count)]
    theirs = lax.ppermute(mine, ("section", "tensor"), swaps)
    return pl.pallas_call(
        functools.partial(unpack_kernel, kinds),
        out_shape=jax.ShapeDtypeStruct((own, feats), F32),
        in_specs=[smem, vmem, vmem],
        out_specs=vmem,
        scratch_shapes=[blocks] * 2,
        compiler_params=pltpu.CompilerParams(vmem_limit_bytes=VMEM_LIMIT),
        name="scored_sums",
    )(me, mine, theirs)


def finish_kernel(
    me_ref, positions_ref, gain_ref, x_ref, later_ref, sums_ref, row_grads_ref, between_ref, within_ref
):
    own = x_ref.shape[0]
    x = x_ref[...].astype(F32)
    hidden = x + sums_ref[:own]
    picks = row_picks(positions_ref[...] - me_ref[0] * own, own)
    last = dot_tn(picks, row_grads_ref[...].astype(BF16))
    cotangent = jnp.where(me_ref[2] == 1, last, later_ref[...].astype(F32))
    inv_x = inv_rms(x)
    scaled = sums_ref[own:] * gain_ref[...].astype(F32)
    mean = jnp.mean(scaled * x, axis=-1, keepdims=True)
    returned = cotangent + inv_x * scaled - x * (inv_x * inv_x * inv_x * mean)
    odd = me_ref[1] == 1
    between_ref[...] = jnp.where(odd, hidden, returned).astype(BF16)
    within_ref[...] = jnp.where(odd, returned, hidden).astype(BF16)


def finish_part(me, positions, gain, x_own, later_own, sums, row_grads):
    vmem = pl.BlockSpec(memory_space=pltpu.VMEM)
    smem = pl.BlockSpec(memory_space=pltpu.SMEM)
    return pl.pallas_call(
        finish_kernel,
        out_shape=[jax.ShapeDtypeStruct(x_own.shape, BF16)] * 2,
        in_specs=[smem] + [vmem] * 6,
        out_specs=[vmem] * 2,
        compiler_params=pltpu.CompilerParams(vmem_limit_bytes=VMEM_LIMIT),
        name="finish",
    )(me, positions, gain, x_own, later_own, sums, row_grads)


def rank_grad(reward_scores, rankings):
    slots = jnp.arange(RESP)
    order_hot = (rankings[0][:, None] == slots[None, :]).astype(F32)
    ordered = jnp.sum(order_hot * reward_scores[None, :], axis=1)
    exp_order = jnp.exp(ordered)
    upper = (slots[:, None] >= slots[None, :]).astype(F32)
    suffix = jnp.sum(exp_order[:, None] * upper, axis=0)
    cumulative = jnp.sum((1.0 / suffix)[None, :] * upper, axis=1)
    grad_order = LOSS_SCALE * (exp_order * cumulative - 1.0)
    return jnp.sum(order_hot * grad_order[:, None], axis=0)


def gather_ring(block):
    count = lax.axis_size("tensor")
    blocks, offsets = [block], [0]
    up = down = block
    for step in range(1, count // 2 + 1):
        up = shift(up, 1)
        blocks.append(up)
        offsets.append(-step)
        if step < count - count // 2:
            down = shift(down, -1)
            blocks.append(down)
            offsets.append(step)
    return blocks, offsets


def scatter_ring(weights, far_mixed, far_back, next_rows, rest_rows, back_offsets, sections):
    far = lax.axis_size("tensor") // 2
    own = far_mixed.shape[0]
    none = jnp.zeros(far_mixed.shape, F32)
    up, down = shift(far_mixed, 1, sections), shift(far_back, -1, sections)
    terms = dict(zip(back_offsets[1:3], terms_of(weights, next_rows, own)))
    up = jnp.concatenate([up.astype(F32), none])
    down = jnp.concatenate([none, down.astype(F32)])
    for left in range(far - 1, 0, -1):
        up = (up.astype(F32) + terms[left].astype(F32)).astype(BF16)
        down = (down.astype(F32) + terms[-left].astype(F32)).astype(BF16)
        if left == far - 1:
            up, rest_rows = lax.optimization_barrier((up, rest_rows))
            terms.update(zip(back_offsets[3:], terms_of(weights, rest_rows, own)))
        up, down = shift(up, 1, sections), shift(down, -1, sections)
    return terms[0].astype(F32) + up.astype(F32) + down.astype(F32)


def sum_rows(value, sections):
    step = 1
    while step < lax.axis_size("tensor"):
        value = value + shift(value, step, sections)
        step *= 2
    return value


def shards(
    section_inputs,
    later_grad,
    attn_gain,
    w_query,
    w_key,
    w_value,
    w_out,
    final_gain,
    reward_head,
    rankings,
    lengths,
):
    x_own = section_inputs[0, 0]
    later_own = later_grad[0, 0]
    own_count = x_own.shape[0]
    tensor_count = lax.axis_size("tensor")
    tensor_pos = lax.axis_index("tensor")
    total_rows = own_count * tensor_count
    length = total_rows // RESP
    weights = (w_query[0], w_key[0], w_value[0], w_out[0])
    at_end = lax.axis_index("section") == lax.axis_size("section") - 1
    positions = jnp.arange(RESP) * length + lengths[0] - 1
    places = positions[:, None].astype(jnp.int32)
    odd = lax.axis_index("section") % 2
    me = jnp.stack([tensor_pos, odd, at_end]).astype(jnp.int32)

    last = lax.axis_size("section") - 1
    blocks, offsets = gather_ring(jnp.concatenate([x_own, later_own]))
    far = tensor_count // 2
    back_offsets = [far, far - 1, 1 - far, *range(2 - far, far - 1)]
    early = early_part(attn_gain, weights, blocks[:-1])

    def inner_section(early, late):
        parts = layer_part(me, attn_gain, weights, early, late, offsets, back_offsets, length)
        sums = scatter_ring(weights, *parts, back_offsets, range(last))
        return sums, jnp.zeros((RESP, x_own.shape[1]), F32)

    def last_section(early, late):
        qkv, rows_part = rows_part_of(
            me, places, attn_gain, weights, early, x_own, late, offsets, length
        )
        rows_hidden = sum_rows(rows_part, [last]).astype(BF16).astype(F32)
        inv_norm = inv_rms(rows_hidden)
        head_vec = final_gain.astype(F32) * reward_head.astype(F32)
        reward_scores = jnp.sum(rows_hidden * inv_norm * head_vec, axis=-1)
        scaled = rank_grad(reward_scores, rankings)[:, None] * head_vec
        row_grads = inv_norm * scaled - rows_hidden * inv_norm**3 * jnp.mean(
            scaled * rows_hidden, axis=-1, keepdims=True
        )
        row_grads = row_grads.astype(BF16).astype(F32)
        back_own = scored_part(
            me, places, row_grads, qkv, weights, tensor_count, length, last
        )
        return jnp.concatenate([jnp.zeros_like(back_own), back_own]), row_grads

    sums, row_grads = lax.cond(at_end, last_section, inner_section, early, blocks[-1])
    between, within = finish_part(me, places, attn_gain, x_own, later_own, sums, row_grads)
    between, within = swap_sections(between, 1), swap_sections(within, 0)
    even = lax.axis_index("section") % 2 == 0
    arrived = jnp.where(even, between, within)
    sent_back = jnp.where(even, within, between)
    return (arrived[None, None], sent_back[None, None])


def solution(mesh):
    return jax.shard_map(
        shards,
        mesh=mesh,
        in_specs=(
            P("section", None, "tensor", None),
            P("section", None, "tensor", None),
            P("section", None),
            P("section", None, "tensor"),
            P("section", None, "tensor"),
            P("section", None, "tensor"),
            P("section", "tensor", None),
            P(),
            P(),
            P(),
            P(),
        ),
        out_specs=(P("section", None, "tensor", None), P("section", None, "tensor", None)),
        check_vma=False,
    )
```

```python
import functools

import jax
import jax.numpy as jnp
from jax import lax
from jax.experimental import pallas as pl
from jax.experimental.pallas import tpu as pltpu
from jax.sharding import PartitionSpec as P

HEAD_DIM = 128
RESP = 8

EPSILON = 1e-06
SOFT_CAP = 50.0
QUERY_SCALE = 1.0 / 12.0
LOSS_SCALE = 64.0

F32 = jnp.float32
BF16 = jnp.bfloat16
VMEM_LIMIT = 24 * 1024 * 1024
BATCH = 8


def shift(value, steps, sections=None):
    count = lax.axis_size("tensor")
    sections = range(lax.axis_size("section")) if sections is None else sections
    pairs = [(s * count + i, s * count + (i + steps) % count) for s in sections for i in range(count)]
    return lax.ppermute(value, ("section", "tensor"), pairs)


def swap_sections(value, first):
    count = lax.axis_size("section")
    pairs = []
    for s in range(first, count - 1, 2):
        pairs += [(s, s + 1), (s + 1, s)]
    return lax.ppermute(value, "section", pairs)


def dot(left, right):
    return lax.dot_general(left, right, (((1,), (0,)), ((), ())), preferred_element_type=F32)


def dot_nt(left, right):
    return lax.dot_general(left, right, (((1,), (1,)), ((), ())), preferred_element_type=F32)


def dot_tn(left, right):
    return lax.dot_general(left, right, (((0,), (0,)), ((), ())), preferred_element_type=F32)


def inv_rms(values):
    return lax.rsqrt(jnp.mean(values * values, axis=-1, keepdims=True) + EPSILON)


def pair_mask(block, length):
    row = lax.broadcasted_iota(jnp.int32, (block, block), 0)
    col = lax.broadcasted_iota(jnp.int32, (block, block), 1)
    return ((row // length == col // length) & (col <= row)).astype(F32)


def positions_of(lengths_ref, length):
    response = lax.broadcasted_iota(jnp.int32, (RESP, 1), 0)
    positions = jnp.zeros((RESP, 1), jnp.int32)
    for i in range(RESP):
        positions = jnp.where(response == i, i * length + lengths_ref[0, i] - 1, positions)
    return positions


def row_picks(positions, rows):
    return (positions == lax.broadcasted_iota(jnp.int32, (RESP, rows), 1)).astype(BF16)


def attention(queries, keys, mask):
    raw = [dot_nt(q, k) for q, k in zip(queries, keys)]
    capped = [jnp.tanh(r * (QUERY_SCALE / SOFT_CAP)) for r in raw]
    exps = [jnp.exp(SOFT_CAP * c) * mask for c in capped]
    sums = [jnp.sum(e, axis=-1, keepdims=True) for e in exps]
    return capped, [e / s for e, s in zip(exps, sums)]


def w_in_of(wq_ref, wk_ref, wv_ref):
    return jnp.concatenate([wq_ref[...], wk_ref[...], wv_ref[...]], axis=1)


def project(gain_ref, w_in, wo_ref, blocks):
    own = blocks[0].shape[0] // 2
    gain = gain_ref[...].astype(F32)
    normed = []
    for block in blocks:
        x_float = block[:own].astype(F32)
        normed.append((x_float * inv_rms(x_float) * gain).astype(BF16))
    normed = jnp.concatenate(normed, axis=0)
    cot = jnp.concatenate([block[own:] for block in blocks], axis=0)
    return dot(normed, w_in).astype(BF16), dot_nt(cot, wo_ref[...]).astype(BF16)


def early_kernel(gain_ref, wq_ref, wk_ref, wv_ref, wo_ref, *refs):
    blocks, out_ref = refs[:-1], refs[-1]
    w_in = w_in_of(wq_ref, wk_ref, wv_ref)
    own = blocks[0].shape[0] // 2
    for first in range(0, len(blocks), BATCH):
        some = blocks[first : first + BATCH]
        parts = project(gain_ref, w_in, wo_ref, some)
        rows = slice(first * own, (first + len(some)) * own)
        out_ref[rows, :] = jnp.concatenate(parts, axis=1)


def early_part(gain, weights, blocks):
    own, feats = blocks[0].shape[0] // 2, blocks[0].shape[1]
    rows, cols = own * len(blocks), sum(w.shape[1] for w in weights[:3]) + weights[3].shape[0]
    vmem = pl.BlockSpec(memory_space=pltpu.VMEM)
    return pl.pallas_call(
        early_kernel,
        out_shape=jax.ShapeDtypeStruct((rows, cols), BF16),
        in_specs=[vmem] * (5 + len(blocks)),
        out_specs=vmem,
        compiler_params=pltpu.CompilerParams(vmem_limit_bytes=VMEM_LIMIT),
        cost_estimate=pl.CostEstimate(
            flops=2 * rows * cols * feats, bytes_accessed=4 * rows * feats, transcendentals=0
        ),
        name="early_rows",
    )(gain, *weights, *blocks)


def place_all(offsets, me_ref, early_ref, late, qkv_ref, grad_ctx=None):
    count = len(offsets)
    cols = qkv_ref.shape[1]
    own = qkv_ref.shape[0] // count
    for i, offset in enumerate(offsets[:-1]):
        rows = pl.ds(place_of(me_ref, offset, count, own), own)
        qkv_ref[rows, :] = early_ref[i * own : (i + 1) * own, :cols]
        if grad_ctx is not None:
            grad_ctx[rows, :] = early_ref[i * own : (i + 1) * own, cols:]
    rows = pl.ds(place_of(me_ref, offsets[-1], count, own), own)
    qkv_ref[rows, :] = late[0]
    if grad_ctx is not None:
        grad_ctx[rows, :] = late[1]


def place_of(me_ref, offset, count, own):
    return pl.multiple_of(lax.rem(me_ref[0] + (offset + count), count) * own, own)


def pairs_of(qkv_ref, length, q_cols, kv_cols):
    block = 2 * length
    spans = [slice(start, start + block) for start in range(0, qkv_ref.shape[0], block)]
    pairs = [(s, h) for s in spans for h in range(0, q_cols, HEAD_DIM)]
    queries = [qkv_ref[s, h : h + HEAD_DIM] for s, h in pairs]
    keys = [qkv_ref[s, q_cols : q_cols + kv_cols] for s, h in pairs]
    values = [qkv_ref[s, q_cols + kv_cols :] for s, h in pairs]
    return spans, pairs, queries, keys, values


def rows_kernel(
    offsets,
    length,
    me_ref,
    lengths_ref,
    gain_ref,
    wq_ref,
    wk_ref,
    wv_ref,
    wo_ref,
    early_ref,
    x_ref,
    late_ref,
    qkv_ref,
    rows_ref,
    context,
):
    own = qkv_ref.shape[0] // len(offsets)
    late = project(gain_ref, w_in_of(wq_ref, wk_ref, wv_ref), wo_ref, [late_ref])
    place_all(offsets, me_ref, early_ref, late, qkv_ref)
    q_cols, kv_cols = wq_ref.shape[1], wk_ref.shape[1]
    _, pairs, queries, keys, values = pairs_of(qkv_ref, length, q_cols, kv_cols)
    _, probs = attention(queries, keys, pair_mask(2 * length, length))
    for (s, h), prob, value in zip(pairs, probs, values):
        context[s, h : h + HEAD_DIM] = dot(prob.astype(BF16), value).astype(BF16)
    positions = positions_of(lengths_ref, length)
    picks = row_picks(positions, qkv_ref.shape[0])
    own_picks = row_picks(positions - me_ref[0] * own, own)
    rows_ref[...] = dot(dot(picks, context[...]).astype(BF16), wo_ref[...]) + dot(
        own_picks, x_ref[...]
    )


def rows_part_of(me, lengths, gain, weights, early, x_own, late, offsets, length):
    own, feats = late.shape[0] // 2, late.shape[1]
    rows = own * len(offsets)
    vmem = pl.BlockSpec(memory_space=pltpu.VMEM)
    smem = pl.BlockSpec(memory_space=pltpu.SMEM)
    cols = sum(w.shape[1] for w in weights[:3])
    return pl.pallas_call(
        functools.partial(rows_kernel, offsets, length),
        out_shape=(
            jax.ShapeDtypeStruct((rows, cols), BF16),
            jax.ShapeDtypeStruct((RESP, feats), F32),
        ),
        in_specs=[smem] * 2 + [vmem] * 8,
        out_specs=[vmem] * 2,
        scratch_shapes=[pltpu.VMEM((rows, weights[0].shape[1]), BF16)],
        compiler_params=pltpu.CompilerParams(vmem_limit_bytes=VMEM_LIMIT),
        name="scored_rows",
    )(me, lengths, gain, *weights, early, x_own, late)


def project_back(turned, wq_ref, wk_ref, wv_ref, wo_ref, mixed_outs, back_outs):
    own, feats = mixed_outs[0].shape[0], wq_ref.shape[0]
    at_mix = turned.shape[1] - wo_ref.shape[0]
    for start in range(0, feats, 256):
        cols = slice(start, start + 256)
        w_in = w_in_of(wq_ref.at[cols], wk_ref.at[cols], wv_ref.at[cols])
        back = dot_nt(turned[:, :at_mix], w_in).astype(BF16)
        mixed = dot(turned[:, at_mix:], wo_ref[:, cols]).astype(BF16)
        for j, (mixed_out, back_out) in enumerate(zip(mixed_outs, back_outs)):
            mixed_out[:, cols] = mixed[j * own : (j + 1) * own]
            back_out[:, cols] = back[j * own : (j + 1) * own]


def layer_kernel(
    offsets,
    back_offsets,
    length,
    me_ref,
    gain_ref,
    wq_ref,
    wk_ref,
    wv_ref,
    wo_ref,
    early_ref,
    late_ref,
    far_mixed_ref,
    far_back_ref,
    next_ref,
    rest_ref,
    qkv,
    grad_ctx,
    work,
    far_rows,
):
    count = len(offsets)
    own = late_ref.shape[0] // 2
    q_cols, kv_cols = wq_ref.shape[1], wk_ref.shape[1]
    late = project(gain_ref, w_in_of(wq_ref, wk_ref, wv_ref), wo_ref, [late_ref])
    place_all(offsets, me_ref, early_ref, late, qkv, grad_ctx)
    spans, pairs, queries, keys, values = pairs_of(qkv, length, q_cols, kv_cols)
    ctxs = [grad_ctx[s, h : h + HEAD_DIM] for s, h in pairs]
    capped, probs = attention(queries, keys, pair_mask(2 * length, length))
    grad_probs = [dot_nt(c, v) for c, v in zip(ctxs, values)]
    means = [jnp.sum(p * g, axis=-1, keepdims=True) for p, g in zip(probs, grad_probs)]
    raws = [
        (p * (g - m) * (1.0 - c * c) * QUERY_SCALE).astype(BF16)
        for p, g, m, c in zip(probs, grad_probs, means, capped)
    ]
    probs = [p.astype(BF16) for p in probs]
    mixes = [dot(p, v).astype(BF16) for p, v in zip(probs, values)]
    grad_queries = [dot(r, k).astype(BF16) for r, k in zip(raws, keys)]
    grad_keys = [dot_tn(r, q) for r, q in zip(raws, queries)]
    grad_values = [dot_tn(p, c) for p, c in zip(probs, ctxs)]
    per = q_cols // HEAD_DIM
    at_keys, at_values, at_mix = q_cols, q_cols + kv_cols, q_cols + 2 * kv_cols
    for (s, h), grad_query, mix in zip(pairs, grad_queries, mixes):
        work[s, h : h + HEAD_DIM] = grad_query
        work[s, at_mix + h : at_mix + h + HEAD_DIM] = mix
    for i, s in enumerate(spans):
        work[s, at_keys:at_values] = sum(grad_keys[i * per : (i + 1) * per]).astype(BF16)
        work[s, at_values:at_mix] = sum(grad_values[i * per : (i + 1) * per]).astype(BF16)
    for i, offset in enumerate(back_offsets):
        rows = work[pl.ds(place_of(me_ref, offset, count, own), own), :]
        if i == 0:
            far_rows[...] = rows
        elif i <= 2:
            next_ref[(i - 1) * own : i * own, :] = rows
        else:
            rest_ref[(i - 3) * own : (i - 2) * own, :] = rows
    project_back(far_rows, wq_ref, wk_ref, wv_ref, wo_ref, [far_mixed_ref], [far_back_ref])


def rest_kernel(wq_ref, wk_ref, wv_ref, wo_ref, rest_ref, *outs):
    own = outs[0].shape[0] // 2
    mixed_outs = [out.at[:own] for out in outs]
    back_outs = [out.at[own:] for out in outs]
    project_back(rest_ref, wq_ref, wk_ref, wv_ref, wo_ref, mixed_outs, back_outs)


def layer_part(me, gain, weights, early, late, offsets, back_offsets, length):
    count = len(offsets)
    own, feats = late.shape[0] // 2, late.shape[1]
    rows = own * count
    vmem = pl.BlockSpec(memory_space=pltpu.VMEM)
    smem = pl.BlockSpec(memory_space=pltpu.SMEM)
    cols, q_cols = sum(w.shape[1] for w in weights[:3]), weights[0].shape[1]
    far_term = jax.ShapeDtypeStruct((own, feats), BF16)
    return pl.pallas_call(
        functools.partial(layer_kernel, offsets, back_offsets, length),
        out_shape=(
            far_term,
            far_term,
            jax.ShapeDtypeStruct((2 * own, cols + q_cols), BF16),
            jax.ShapeDtypeStruct((rows - 3 * own, cols + q_cols), BF16),
        ),
        in_specs=[smem] + [vmem] * 7,
        out_specs=[vmem] * 4,
        scratch_shapes=[
            pltpu.VMEM((rows, cols), BF16),
            pltpu.VMEM((rows, q_cols), BF16),
            pltpu.VMEM((rows, cols + q_cols), BF16),
            pltpu.VMEM((own, cols + q_cols), BF16),
        ],
        compiler_params=pltpu.CompilerParams(vmem_limit_bytes=VMEM_LIMIT),
        name="layer_both_ways",
    )(me, gain, *weights, early, late)


def terms_of(weights, turned, own):
    count, feats = turned.shape[0] // own, weights[0].shape[0]
    vmem = pl.BlockSpec(memory_space=pltpu.VMEM)
    return pl.pallas_call(
        rest_kernel,
        out_shape=[jax.ShapeDtypeStruct((2 * own, feats), BF16)] * count,
        in_specs=[vmem] * 5,
        out_specs=[vmem] * count,
        compiler_params=pltpu.CompilerParams(vmem_limit_bytes=VMEM_LIMIT),
        cost_estimate=pl.CostEstimate(
            flops=2 * turned.size * feats, bytes_accessed=0, transcendentals=0
        ),
        name="rest_of_terms",
    )(*weights, turned)


def scored_kernel(
    count,
    length,
    lengths_ref,
    row_grads_ref,
    qkv_ref,
    wq_ref,
    wk_ref,
    wv_ref,
    wo_ref,
    parcels_ref,
    packed,
):
    rows = qkv_ref.shape[0]
    feats = wq_ref.shape[0]
    own = rows // count
    q_cols, kv_cols = wq_ref.shape[1], wk_ref.shape[1]
    positions = positions_of(lengths_ref, length)
    picks = row_picks(positions, rows)
    row = lax.broadcasted_iota(jnp.int32, (RESP, rows), 0)
    col = lax.broadcasted_iota(jnp.int32, (RESP, rows), 1)
    mask = ((col // length == row) & (col <= positions)).astype(F32)
    query_all = dot(picks, qkv_ref[:, :q_cols]).astype(BF16)
    ctx_all = dot_nt(row_grads_ref[...].astype(BF16), wo_ref[...]).astype(BF16)
    keys = qkv_ref[:, q_cols : q_cols + kv_cols]
    values = qkv_ref[:, q_cols + kv_cols :]
    heads = range(0, q_cols, HEAD_DIM)
    queries = [query_all[:, h : h + HEAD_DIM] for h in heads]
    ctxs = [ctx_all[:, h : h + HEAD_DIM] for h in heads]
    capped, probs = attention(queries, [keys] * len(heads), mask)
    raws = []
    for prob, cap, ctx in zip(probs, capped, ctxs):
        grad_prob = dot_nt(ctx, values)
        grad_score = prob * (grad_prob - jnp.sum(prob * grad_prob, axis=-1, keepdims=True))
        raws.append((grad_score * (1.0 - cap * cap) * QUERY_SCALE).astype(BF16))
    grad_query = jnp.concatenate([dot(raw, keys) for raw in raws], axis=1).astype(BF16)
    vectors = [dot_nt(q, wk_ref[...]) for q in queries] + [dot_nt(c, wv_ref[...]) for c in ctxs]
    vectors.append(dot_nt(grad_query, wq_ref[...]))
    fold_row = lax.broadcasted_iota(jnp.int32, (rows, length), 0)
    fold_col = lax.broadcasted_iota(jnp.int32, (rows, length), 1)
    fold = (fold_row % length == fold_col).astype(BF16)
    shares = [dot(c, fold) for c in raws + [p.astype(BF16) for p in probs] + [picks]]
    owners = length // own
    lanes, slots, width, half = parcel_shape(len(vectors), feats, owners)
    stride = owners * slots
    packed[...] = jnp.zeros(packed.shape, F32)
    for i in range(len(vectors) * feats // lanes):
        vector, place = divmod(i * lanes, feats)
        owner, block = divmod(i, half)
        slot, at = divmod(block * lanes, width)
        packed[at // lanes, pl.ds(owner * slots + slot, RESP, stride=stride), :] = vectors[vector][
            :, place : place + lanes
        ]
    per = lanes // own
    for owner in range(owners):
        for first in range(0, len(shares), per):
            slot, at = divmod((half + first // per) * lanes, width)
            some = [s[:, owner * own : (owner + 1) * own] for s in shares[first : first + per]]
            some += [jnp.zeros((RESP, own), F32)] * (per - len(some))
            packed[at // lanes, pl.ds(owner * slots + slot, RESP, stride=stride), :] = (
                jnp.concatenate(some, axis=1)
            )
    for i in range(width // lanes):
        parcels_ref[:, i * lanes : (i + 1) * lanes] = packed[i].astype(BF16)


def parcel_shape(kinds, feats, owners):
    lanes, slots = 128, 8
    half = kinds * feats // lanes // owners
    blocks = half + 2
    return lanes, slots, -(-blocks // slots) * lanes, half


def unpack_kernel(kinds, me_ref, mine_ref, theirs_ref, out_ref, mine, theirs):
    own, feats = out_ref.shape
    owners = 2
    lanes, slots, width, half = parcel_shape(kinds, feats, owners)
    count = mine_ref.shape[0] // slots
    for i in range(width // lanes):
        mine[i] = mine_ref[:, i * lanes : (i + 1) * lanes].astype(F32)
        theirs[i] = theirs_ref[:, i * lanes : (i + 1) * lanes].astype(F32)
    second = lax.rem(me_ref[0], owners) == 1

    def block_of(ref, block):
        slot, at = divmod(block * lanes, width)
        return ref[at // lanes, pl.ds(slot, count, stride=slots), :]

    per = lanes // own
    shares = [block_of(mine, half + k // per)[:, k % per * own : (k % per + 1) * own] for k in range(kinds)]
    shares = jnp.concatenate(shares, axis=0).astype(BF16)
    for place in range(0, feats, lanes):
        parts = []
        for vector in range(kinds):
            owner, block = divmod((vector * feats + place) // lanes, half)
            here, there = block_of(mine, block), block_of(theirs, block)
            swap = second if owner == 0 else jnp.logical_not(second)
            parts.append(jnp.where(swap, there, here))
        out_ref[:, place : place + lanes] = dot_tn(shares, jnp.concatenate(parts, axis=0).astype(BF16))


def scored_part(me, lengths, row_grads, qkv, weights, count, length, section):
    feats = row_grads.shape[1]
    own = qkv.shape[0] // count
    vmem = pl.BlockSpec(memory_space=pltpu.VMEM)
    smem = pl.BlockSpec(memory_space=pltpu.SMEM)
    kinds = 2 * (weights[0].shape[1] // HEAD_DIM) + 1
    lanes, slots, width, _ = parcel_shape(kinds, feats, length // own)
    shape = (count * slots, width)
    blocks = pltpu.VMEM((width // lanes, count * slots, lanes), F32)
    parcels = pl.pallas_call(
        functools.partial(scored_kernel, count, length),
        out_shape=jax.ShapeDtypeStruct(shape, BF16),
        in_specs=[smem] + [vmem] * 6,
        out_specs=vmem,
        scratch_shapes=[blocks],
        compiler_params=pltpu.CompilerParams(vmem_limit_bytes=VMEM_LIMIT),
        name="scored_backward",
    )(lengths, row_grads, qkv, *weights)
    mine = lax.all_to_all(parcels.reshape(count, slots, width), "tensor", 0, 0).reshape(shape)
    swaps = [(section * count + i, section * count + (i ^ 1)) for i in range(count)]
    theirs = lax.ppermute(mine, ("section", "tensor"), swaps)
    return pl.pallas_call(
        functools.partial(unpack_kernel, kinds),
        out_shape=jax.ShapeDtypeStruct((own, feats), F32),
        in_specs=[smem, vmem, vmem],
        out_specs=vmem,
        scratch_shapes=[blocks] * 2,
        compiler_params=pltpu.CompilerParams(vmem_limit_bytes=VMEM_LIMIT),
        name="scored_sums",
    )(me, mine, theirs)


def finish_kernel(
    length,
    me_ref,
    lengths_ref,
    gain_ref,
    x_ref,
    later_ref,
    sums_ref,
    row_grads_ref,
    between_ref,
    within_ref,
):
    own = x_ref.shape[0]
    x = x_ref[...].astype(F32)
    hidden = x + sums_ref[:own]
    picks = row_picks(positions_of(lengths_ref, length) - me_ref[0] * own, own)
    last = dot_tn(picks, row_grads_ref[...].astype(BF16))
    cotangent = jnp.where(me_ref[2] == 1, last, later_ref[...].astype(F32))
    inv_x = inv_rms(x)
    scaled = sums_ref[own:] * gain_ref[...].astype(F32)
    mean = jnp.mean(scaled * x, axis=-1, keepdims=True)
    returned = cotangent + inv_x * scaled - x * (inv_x * inv_x * inv_x * mean)
    odd = me_ref[1] == 1
    between_ref[...] = jnp.where(odd, hidden, returned).astype(BF16)
    within_ref[...] = jnp.where(odd, returned, hidden).astype(BF16)


def finish_part(me, lengths, gain, x_own, later_own, sums, row_grads, length):
    vmem = pl.BlockSpec(memory_space=pltpu.VMEM)
    smem = pl.BlockSpec(memory_space=pltpu.SMEM)
    return pl.pallas_call(
        functools.partial(finish_kernel, length),
        out_shape=[jax.ShapeDtypeStruct(x_own.shape, BF16)] * 2,
        in_specs=[smem] * 2 + [vmem] * 5,
        out_specs=[vmem] * 2,
        compiler_params=pltpu.CompilerParams(vmem_limit_bytes=VMEM_LIMIT),
        name="finish",
    )(me, lengths, gain, x_own, later_own, sums, row_grads)


def rank_grad(reward_scores, rankings):
    slots = jnp.arange(RESP)
    order_hot = (rankings[0][:, None] == slots[None, :]).astype(F32)
    ordered = jnp.sum(order_hot * reward_scores[None, :], axis=1)
    exp_order = jnp.exp(ordered)
    upper = (slots[:, None] >= slots[None, :]).astype(F32)
    suffix = jnp.sum(exp_order[:, None] * upper, axis=0)
    cumulative = jnp.sum((1.0 / suffix)[None, :] * upper, axis=1)
    grad_order = LOSS_SCALE * (exp_order * cumulative - 1.0)
    return jnp.sum(order_hot * grad_order[:, None], axis=0)


def gather_ring(block):
    count = lax.axis_size("tensor")
    blocks, offsets = [block], [0]
    up = down = block
    for step in range(1, count // 2 + 1):
        up = shift(up, 1)
        blocks.append(up)
        offsets.append(-step)
        if step < count - count // 2:
            down = shift(down, -1)
            blocks.append(down)
            offsets.append(step)
    return blocks, offsets


def scatter_ring(weights, far_mixed, far_back, next_rows, rest_rows, back_offsets, sections):
    far = lax.axis_size("tensor") // 2
    own = far_mixed.shape[0]
    none = jnp.zeros(far_mixed.shape, F32)
    up, down = shift(far_mixed, 1, sections), shift(far_back, -1, sections)
    terms = dict(zip(back_offsets[1:3], terms_of(weights, next_rows, own)))
    up = jnp.concatenate([up.astype(F32), none])
    down = jnp.concatenate([none, down.astype(F32)])
    for left in range(far - 1, 0, -1):
        up = (up.astype(F32) + terms[left].astype(F32)).astype(BF16)
        down = (down.astype(F32) + terms[-left].astype(F32)).astype(BF16)
        if left == far - 1:
            up, rest_rows = lax.optimization_barrier((up, rest_rows))
            terms.update(zip(back_offsets[3:], terms_of(weights, rest_rows, own)))
        up, down = shift(up, 1, sections), shift(down, -1, sections)
    return terms[0].astype(F32) + up.astype(F32) + down.astype(F32)


def sum_rows(value, sections):
    step = 1
    while step < lax.axis_size("tensor"):
        value = value + shift(value, step, sections)
        step *= 2
    return value


def shards(
    section_inputs,
    later_grad,
    attn_gain,
    w_query,
    w_key,
    w_value,
    w_out,
    final_gain,
    reward_head,
    rankings,
    lengths,
):
    x_own = section_inputs[0, 0]
    later_own = later_grad[0, 0]
    own_count = x_own.shape[0]
    tensor_count = lax.axis_size("tensor")
    tensor_pos = lax.axis_index("tensor")
    total_rows = own_count * tensor_count
    length = total_rows // RESP
    weights = (w_query[0], w_key[0], w_value[0], w_out[0])
    at_end = lax.axis_index("section") == lax.axis_size("section") - 1
    odd = lax.axis_index("section") % 2
    me = jnp.stack([tensor_pos, odd, at_end]).astype(jnp.int32)

    last = lax.axis_size("section") - 1
    blocks, offsets = gather_ring(jnp.concatenate([x_own, later_own]))
    far = tensor_count // 2
    back_offsets = [far, far - 1, 1 - far, *range(2 - far, far - 1)]
    early = early_part(attn_gain, weights, blocks[:-1])

    def inner_section(early, late):
        parts = layer_part(me, attn_gain, weights, early, late, offsets, back_offsets, length)
        sums = scatter_ring(weights, *parts, back_offsets, range(last))
        return sums, jnp.zeros((RESP, x_own.shape[1]), F32)

    def last_section(early, late):
        qkv, rows_part = rows_part_of(
            me, lengths, attn_gain, weights, early, x_own, late, offsets, length
        )
        rows_hidden = sum_rows(rows_part, [last]).astype(BF16).astype(F32)
        inv_norm = inv_rms(rows_hidden)
        head_vec = final_gain.astype(F32) * reward_head.astype(F32)
        reward_scores = jnp.sum(rows_hidden * inv_norm * head_vec, axis=-1)
        scaled = rank_grad(reward_scores, rankings)[:, None] * head_vec
        row_grads = inv_norm * scaled - rows_hidden * inv_norm**3 * jnp.mean(
            scaled * rows_hidden, axis=-1, keepdims=True
        )
        row_grads = row_grads.astype(BF16).astype(F32)
        back_own = scored_part(
            me, lengths, row_grads, qkv, weights, tensor_count, length, last
        )
        return jnp.concatenate([jnp.zeros_like(back_own), back_own]), row_grads

    sums, row_grads = lax.cond(at_end, last_section, inner_section, early, blocks[-1])
    between, within = finish_part(
        me, lengths, attn_gain, x_own, later_own, sums, row_grads, length
    )
    between, within = swap_sections(between, 1), swap_sections(within, 0)
    even = lax.axis_index("section") % 2 == 0
    arrived = jnp.where(even, between, within)
    sent_back = jnp.where(even, within, between)
    return (arrived[None, None], sent_back[None, None])


def solution(mesh):
    return jax.shard_map(
        shards,
        mesh=mesh,
        in_specs=(
            P("section", None, "tensor", None),
            P("section", None, "tensor", None),
            P("section", None),
            P("section", None, "tensor"),
            P("section", None, "tensor"),
            P("section", None, "tensor"),
            P("section", "tensor", None),
            P(),
            P(),
            P(),
            P(),
        ),
        out_specs=(P("section", None, "tensor", None), P("section", None, "tensor", None)),
        check_vma=False,
    )
```

```python
import functools

import jax
import jax.numpy as jnp
from jax import lax
from jax.experimental import pallas as pl
from jax.experimental.pallas import tpu as pltpu
from jax.sharding import PartitionSpec as P

HEAD_DIM = 128
RESP = 8

EPSILON = 1e-06
SOFT_CAP = 50.0
QUERY_SCALE = 1.0 / 12.0
LOSS_SCALE = 64.0

F32 = jnp.float32
BF16 = jnp.bfloat16
VMEM_LIMIT = 24 * 1024 * 1024
BATCH = 8


def shift(value, steps, sections=None):
    count = lax.axis_size("tensor")
    sections = range(lax.axis_size("section")) if sections is None else sections
    pairs = [(s * count + i, s * count + (i + steps) % count) for s in sections for i in range(count)]
    return lax.ppermute(value, ("section", "tensor"), pairs)


def swap_sections(value, first):
    count = lax.axis_size("section")
    pairs = []
    for s in range(first, count - 1, 2):
        pairs += [(s, s + 1), (s + 1, s)]
    return lax.ppermute(value, "section", pairs)


def dot(left, right):
    return lax.dot_general(left, right, (((1,), (0,)), ((), ())), preferred_element_type=F32)


def dot_nt(left, right):
    return lax.dot_general(left, right, (((1,), (1,)), ((), ())), preferred_element_type=F32)


def dot_tn(left, right):
    return lax.dot_general(left, right, (((0,), (0,)), ((), ())), preferred_element_type=F32)


def inv_rms(values):
    return lax.rsqrt(jnp.mean(values * values, axis=-1, keepdims=True) + EPSILON)


def pair_mask(block, length):
    row = lax.broadcasted_iota(jnp.int32, (block, block), 0)
    col = lax.broadcasted_iota(jnp.int32, (block, block), 1)
    return ((row // length == col // length) & (col <= row)).astype(F32)


def row_picks(positions, rows):
    return (positions == lax.broadcasted_iota(jnp.int32, (RESP, rows), 1)).astype(BF16)


def attention(queries, keys, mask):
    raw = [dot_nt(q, k) for q, k in zip(queries, keys)]
    capped = [jnp.tanh(r * (QUERY_SCALE / SOFT_CAP)) for r in raw]
    exps = [jnp.exp(SOFT_CAP * c) * mask for c in capped]
    sums = [jnp.sum(e, axis=-1, keepdims=True) for e in exps]
    return capped, [e / s for e, s in zip(exps, sums)]


def w_in_of(wq_ref, wk_ref, wv_ref):
    return jnp.concatenate([wq_ref[...], wk_ref[...], wv_ref[...]], axis=1)


def project(gain_ref, w_in, wo_ref, blocks):
    own = blocks[0].shape[0] // 2
    gain = gain_ref[...].astype(F32)
    normed = []
    for block in blocks:
        x_float = block[:own].astype(F32)
        normed.append((x_float * inv_rms(x_float) * gain).astype(BF16))
    normed = jnp.concatenate(normed, axis=0)
    cot = jnp.concatenate([block[own:] for block in blocks], axis=0)
    return dot(normed, w_in).astype(BF16), dot_nt(cot, wo_ref[...]).astype(BF16)


def early_kernel(gain_ref, wq_ref, wk_ref, wv_ref, wo_ref, *refs):
    blocks, out_ref = refs[:-1], refs[-1]
    w_in = w_in_of(wq_ref, wk_ref, wv_ref)
    own = blocks[0].shape[0] // 2
    for first in range(0, len(blocks), BATCH):
        some = blocks[first : first + BATCH]
        parts = project(gain_ref, w_in, wo_ref, some)
        rows = slice(first * own, (first + len(some)) * own)
        out_ref[rows, :] = jnp.concatenate(parts, axis=1)


def early_part(gain, weights, blocks):
    own, feats = blocks[0].shape[0] // 2, blocks[0].shape[1]
    rows, cols = own * len(blocks), sum(w.shape[1] for w in weights[:3]) + weights[3].shape[0]
    vmem = pl.BlockSpec(memory_space=pltpu.VMEM)
    return pl.pallas_call(
        early_kernel,
        out_shape=jax.ShapeDtypeStruct((rows, cols), BF16),
        in_specs=[vmem] * (5 + len(blocks)),
        out_specs=vmem,
        compiler_params=pltpu.CompilerParams(vmem_limit_bytes=VMEM_LIMIT),
        cost_estimate=pl.CostEstimate(
            flops=2 * rows * cols * feats, bytes_accessed=4 * rows * feats, transcendentals=0
        ),
        name="early_rows",
    )(gain, *weights, *blocks)


def place_all(offsets, me_ref, early_ref, late, qkv_ref, grad_ctx=None):
    count = len(offsets)
    cols = qkv_ref.shape[1]
    own = qkv_ref.shape[0] // count
    for i, offset in enumerate(offsets[:-1]):
        rows = pl.ds(place_of(me_ref, offset, count, own), own)
        qkv_ref[rows, :] = early_ref[i * own : (i + 1) * own, :cols]
        if grad_ctx is not None:
            grad_ctx[rows, :] = early_ref[i * own : (i + 1) * own, cols:]
    rows = pl.ds(place_of(me_ref, offsets[-1], count, own), own)
    qkv_ref[rows, :] = late[0]
    if grad_ctx is not None:
        grad_ctx[rows, :] = late[1]


def place_of(me_ref, offset, count, own):
    return pl.multiple_of(lax.rem(me_ref[0] + (offset + count), count) * own, own)


def pairs_of(qkv_ref, length, q_cols, kv_cols):
    block = 2 * length
    spans = [slice(start, start + block) for start in range(0, qkv_ref.shape[0], block)]
    pairs = [(s, h) for s in spans for h in range(0, q_cols, HEAD_DIM)]
    queries = [qkv_ref[s, h : h + HEAD_DIM] for s, h in pairs]
    keys = [qkv_ref[s, q_cols : q_cols + kv_cols] for s, h in pairs]
    values = [qkv_ref[s, q_cols + kv_cols :] for s, h in pairs]
    return spans, pairs, queries, keys, values


def rows_kernel(
    offsets,
    length,
    me_ref,
    positions_ref,
    gain_ref,
    wq_ref,
    wk_ref,
    wv_ref,
    wo_ref,
    early_ref,
    x_ref,
    late_ref,
    qkv_ref,
    rows_ref,
    context,
):
    own = qkv_ref.shape[0] // len(offsets)
    late = project(gain_ref, w_in_of(wq_ref, wk_ref, wv_ref), wo_ref, [late_ref])
    place_all(offsets, me_ref, early_ref, late, qkv_ref)
    q_cols, kv_cols = wq_ref.shape[1], wk_ref.shape[1]
    _, pairs, queries, keys, values = pairs_of(qkv_ref, length, q_cols, kv_cols)
    _, probs = attention(queries, keys, pair_mask(2 * length, length))
    for (s, h), prob, value in zip(pairs, probs, values):
        context[s, h : h + HEAD_DIM] = dot(prob.astype(BF16), value).astype(BF16)
    picks = row_picks(positions_ref[...], qkv_ref.shape[0])
    own_picks = row_picks(positions_ref[...] - me_ref[0] * own, own)
    rows_ref[...] = dot(dot(picks, context[...]).astype(BF16), wo_ref[...]) + dot(
        own_picks, x_ref[...]
    )


def rows_part_of(me, positions, gain, weights, early, x_own, late, offsets, length):
    own, feats = late.shape[0] // 2, late.shape[1]
    rows = own * len(offsets)
    vmem = pl.BlockSpec(memory_space=pltpu.VMEM)
    smem = pl.BlockSpec(memory_space=pltpu.SMEM)
    cols = sum(w.shape[1] for w in weights[:3])
    return pl.pallas_call(
        functools.partial(rows_kernel, offsets, length),
        out_shape=(
            jax.ShapeDtypeStruct((rows, cols), BF16),
            jax.ShapeDtypeStruct((RESP, feats), F32),
        ),
        in_specs=[smem] + [vmem] * 9,
        out_specs=[vmem] * 2,
        scratch_shapes=[pltpu.VMEM((rows, weights[0].shape[1]), BF16)],
        compiler_params=pltpu.CompilerParams(vmem_limit_bytes=VMEM_LIMIT),
        name="scored_rows",
    )(me, positions, gain, *weights, early, x_own, late)


def project_back(turned, wq_ref, wk_ref, wv_ref, wo_ref, mixed_outs, back_outs):
    own, feats = mixed_outs[0].shape[0], wq_ref.shape[0]
    at_mix = turned.shape[1] - wo_ref.shape[0]
    for start in range(0, feats, 768):
        cols = slice(start, start + 768)
        w_in = w_in_of(wq_ref.at[cols], wk_ref.at[cols], wv_ref.at[cols])
        back = dot_nt(turned[:, :at_mix], w_in).astype(BF16)
        mixed = dot(turned[:, at_mix:], wo_ref[:, cols]).astype(BF16)
        for j, (mixed_out, back_out) in enumerate(zip(mixed_outs, back_outs)):
            mixed_out[:, cols] = mixed[j * own : (j + 1) * own]
            back_out[:, cols] = back[j * own : (j + 1) * own]


def layer_kernel(
    offsets,
    back_offsets,
    length,
    me_ref,
    gain_ref,
    wq_ref,
    wk_ref,
    wv_ref,
    wo_ref,
    early_ref,
    late_ref,
    far_mixed_ref,
    far_back_ref,
    next_ref,
    rest_ref,
    qkv,
    grad_ctx,
    work,
    far_rows,
):
    count = len(offsets)
    own = late_ref.shape[0] // 2
    q_cols, kv_cols = wq_ref.shape[1], wk_ref.shape[1]
    late = project(gain_ref, w_in_of(wq_ref, wk_ref, wv_ref), wo_ref, [late_ref])
    place_all(offsets, me_ref, early_ref, late, qkv, grad_ctx)
    spans, pairs, queries, keys, values = pairs_of(qkv, length, q_cols, kv_cols)
    ctxs = [grad_ctx[s, h : h + HEAD_DIM] for s, h in pairs]
    capped, probs = attention(queries, keys, pair_mask(2 * length, length))
    grad_probs = [dot_nt(c, v) for c, v in zip(ctxs, values)]
    means = [jnp.sum(p * g, axis=-1, keepdims=True) for p, g in zip(probs, grad_probs)]
    raws = [
        (p * (g - m) * (1.0 - c * c) * QUERY_SCALE).astype(BF16)
        for p, g, m, c in zip(probs, grad_probs, means, capped)
    ]
    probs = [p.astype(BF16) for p in probs]
    mixes = [dot(p, v).astype(BF16) for p, v in zip(probs, values)]
    grad_queries = [dot(r, k).astype(BF16) for r, k in zip(raws, keys)]
    grad_keys = [dot_tn(r, q) for r, q in zip(raws, queries)]
    grad_values = [dot_tn(p, c) for p, c in zip(probs, ctxs)]
    per = q_cols // HEAD_DIM
    at_keys, at_values, at_mix = q_cols, q_cols + kv_cols, q_cols + 2 * kv_cols
    for (s, h), grad_query, mix in zip(pairs, grad_queries, mixes):
        work[s, h : h + HEAD_DIM] = grad_query
        work[s, at_mix + h : at_mix + h + HEAD_DIM] = mix
    for i, s in enumerate(spans):
        work[s, at_keys:at_values] = sum(grad_keys[i * per : (i + 1) * per]).astype(BF16)
        work[s, at_values:at_mix] = sum(grad_values[i * per : (i + 1) * per]).astype(BF16)
    for i, offset in enumerate(back_offsets):
        rows = work[pl.ds(place_of(me_ref, offset, count, own), own), :]
        if i == 0:
            far_rows[...] = rows
        elif i <= 2:
            next_ref[(i - 1) * own : i * own, :] = rows
        else:
            rest_ref[(i - 3) * own : (i - 2) * own, :] = rows
    project_back(far_rows, wq_ref, wk_ref, wv_ref, wo_ref, [far_mixed_ref], [far_back_ref])


def rest_kernel(wq_ref, wk_ref, wv_ref, wo_ref, rest_ref, *outs):
    own = outs[0].shape[0] // 2
    mixed_outs = [out.at[:own] for out in outs]
    back_outs = [out.at[own:] for out in outs]
    project_back(rest_ref, wq_ref, wk_ref, wv_ref, wo_ref, mixed_outs, back_outs)


def layer_part(me, gain, weights, early, late, offsets, back_offsets, length):
    count = len(offsets)
    own, feats = late.shape[0] // 2, late.shape[1]
    rows = own * count
    vmem = pl.BlockSpec(memory_space=pltpu.VMEM)
    smem = pl.BlockSpec(memory_space=pltpu.SMEM)
    cols, q_cols = sum(w.shape[1] for w in weights[:3]), weights[0].shape[1]
    far_term = jax.ShapeDtypeStruct((own, feats), BF16)
    return pl.pallas_call(
        functools.partial(layer_kernel, offsets, back_offsets, length),
        out_shape=(
            far_term,
            far_term,
            jax.ShapeDtypeStruct((2 * own, cols + q_cols), BF16),
            jax.ShapeDtypeStruct((rows - 3 * own, cols + q_cols), BF16),
        ),
        in_specs=[smem] + [vmem] * 7,
        out_specs=[vmem] * 4,
        scratch_shapes=[
            pltpu.VMEM((rows, cols), BF16),
            pltpu.VMEM((rows, q_cols), BF16),
            pltpu.VMEM((rows, cols + q_cols), BF16),
            pltpu.VMEM((own, cols + q_cols), BF16),
        ],
        compiler_params=pltpu.CompilerParams(vmem_limit_bytes=VMEM_LIMIT),
        name="layer_both_ways",
    )(me, gain, *weights, early, late)


def terms_of(weights, turned, own):
    count, feats = turned.shape[0] // own, weights[0].shape[0]
    vmem = pl.BlockSpec(memory_space=pltpu.VMEM)
    return pl.pallas_call(
        rest_kernel,
        out_shape=[jax.ShapeDtypeStruct((2 * own, feats), BF16)] * count,
        in_specs=[vmem] * 5,
        out_specs=[vmem] * count,
        compiler_params=pltpu.CompilerParams(vmem_limit_bytes=VMEM_LIMIT),
        cost_estimate=pl.CostEstimate(
            flops=2 * turned.size * feats, bytes_accessed=0, transcendentals=0
        ),
        name="rest_of_terms",
    )(*weights, turned)


def scored_kernel(
    count,
    length,
    positions_ref,
    row_grads_ref,
    qkv_ref,
    wq_ref,
    wk_ref,
    wv_ref,
    wo_ref,
    parcels_ref,
    packed,
):
    rows = qkv_ref.shape[0]
    feats = wq_ref.shape[0]
    own = rows // count
    q_cols, kv_cols = wq_ref.shape[1], wk_ref.shape[1]
    positions = positions_ref[...]
    picks = row_picks(positions, rows)
    row = lax.broadcasted_iota(jnp.int32, (RESP, rows), 0)
    col = lax.broadcasted_iota(jnp.int32, (RESP, rows), 1)
    mask = ((col // length == row) & (col <= positions)).astype(F32)
    query_all = dot(picks, qkv_ref[:, :q_cols]).astype(BF16)
    ctx_all = dot_nt(row_grads_ref[...].astype(BF16), wo_ref[...]).astype(BF16)
    keys = qkv_ref[:, q_cols : q_cols + kv_cols]
    values = qkv_ref[:, q_cols + kv_cols :]
    heads = range(0, q_cols, HEAD_DIM)
    queries = [query_all[:, h : h + HEAD_DIM] for h in heads]
    ctxs = [ctx_all[:, h : h + HEAD_DIM] for h in heads]
    capped, probs = attention(queries, [keys] * len(heads), mask)
    raws = []
    for prob, cap, ctx in zip(probs, capped, ctxs):
        grad_prob = dot_nt(ctx, values)
        grad_score = prob * (grad_prob - jnp.sum(prob * grad_prob, axis=-1, keepdims=True))
        raws.append((grad_score * (1.0 - cap * cap) * QUERY_SCALE).astype(BF16))
    grad_query = jnp.concatenate([dot(raw, keys) for raw in raws], axis=1).astype(BF16)
    vectors = [dot_nt(q, wk_ref[...]) for q in queries] + [dot_nt(c, wv_ref[...]) for c in ctxs]
    vectors.append(dot_nt(grad_query, wq_ref[...]))
    fold_row = lax.broadcasted_iota(jnp.int32, (rows, length), 0)
    fold_col = lax.broadcasted_iota(jnp.int32, (rows, length), 1)
    fold = (fold_row % length == fold_col).astype(BF16)
    shares = [dot(c, fold) for c in raws + [p.astype(BF16) for p in probs] + [picks]]
    owners = length // own
    lanes, slots, width, half = parcel_shape(len(vectors), feats, owners)
    stride = owners * slots
    packed[...] = jnp.zeros(packed.shape, F32)
    for i in range(len(vectors) * feats // lanes):
        vector, place = divmod(i * lanes, feats)
        owner, block = divmod(i, half)
        slot, at = divmod(block * lanes, width)
        packed[at // lanes, pl.ds(owner * slots + slot, RESP, stride=stride), :] = vectors[vector][
            :, place : place + lanes
        ]
    per = lanes // own
    for owner in range(owners):
        for first in range(0, len(shares), per):
            slot, at = divmod((half + first // per) * lanes, width)
            some = [s[:, owner * own : (owner + 1) * own] for s in shares[first : first + per]]
            some += [jnp.zeros((RESP, own), F32)] * (per - len(some))
            packed[at // lanes, pl.ds(owner * slots + slot, RESP, stride=stride), :] = (
                jnp.concatenate(some, axis=1)
            )
    for i in range(width // lanes):
        parcels_ref[:, i * lanes : (i + 1) * lanes] = packed[i].astype(BF16)


def parcel_shape(kinds, feats, owners):
    lanes, slots = 128, 8
    half = kinds * feats // lanes // owners
    blocks = half + 2
    return lanes, slots, -(-blocks // slots) * lanes, half


def unpack_kernel(kinds, me_ref, mine_ref, theirs_ref, out_ref, mine, theirs):
    own, feats = out_ref.shape
    owners = 2
    lanes, slots, width, half = parcel_shape(kinds, feats, owners)
    count = mine_ref.shape[0] // slots
    for i in range(width // lanes):
        mine[i] = mine_ref[:, i * lanes : (i + 1) * lanes].astype(F32)
        theirs[i] = theirs_ref[:, i * lanes : (i + 1) * lanes].astype(F32)
    second = lax.rem(me_ref[0], owners) == 1

    def block_of(ref, block):
        slot, at = divmod(block * lanes, width)
        return ref[at // lanes, pl.ds(slot, count, stride=slots), :]

    per = lanes // own
    shares = [block_of(mine, half + k // per)[:, k % per * own : (k % per + 1) * own] for k in range(kinds)]
    shares = jnp.concatenate(shares, axis=0).astype(BF16)
    for place in range(0, feats, lanes):
        parts = []
        for vector in range(kinds):
            owner, block = divmod((vector * feats + place) // lanes, half)
            here, there = block_of(mine, block), block_of(theirs, block)
            swap = second if owner == 0 else jnp.logical_not(second)
            parts.append(jnp.where(swap, there, here))
        out_ref[:, place : place + lanes] = dot_tn(shares, jnp.concatenate(parts, axis=0).astype(BF16))


def scored_part(me, positions, row_grads, qkv, weights, count, length, section):
    feats = row_grads.shape[1]
    own = qkv.shape[0] // count
    vmem = pl.BlockSpec(memory_space=pltpu.VMEM)
    smem = pl.BlockSpec(memory_space=pltpu.SMEM)
    kinds = 2 * (weights[0].shape[1] // HEAD_DIM) + 1
    lanes, slots, width, _ = parcel_shape(kinds, feats, length // own)
    shape = (count * slots, width)
    blocks = pltpu.VMEM((width // lanes, count * slots, lanes), F32)
    parcels = pl.pallas_call(
        functools.partial(scored_kernel, count, length),
        out_shape=jax.ShapeDtypeStruct(shape, BF16),
        in_specs=[vmem] * 7,
        out_specs=vmem,
        scratch_shapes=[blocks],
        compiler_params=pltpu.CompilerParams(vmem_limit_bytes=VMEM_LIMIT),
        name="scored_backward",
    )(positions, row_grads, qkv, *weights)
    mine = lax.all_to_all(parcels.reshape(count, slots, width), "tensor", 0, 0).reshape(shape)
    swaps = [(section * count + i, section * count + (i ^ 1)) for i in range(count)]
    theirs = lax.ppermute(mine, ("section", "tensor"), swaps)
    return pl.pallas_call(
        functools.partial(unpack_kernel, kinds),
        out_shape=jax.ShapeDtypeStruct((own, feats), F32),
        in_specs=[smem, vmem, vmem],
        out_specs=vmem,
        scratch_shapes=[blocks] * 2,
        compiler_params=pltpu.CompilerParams(vmem_limit_bytes=VMEM_LIMIT),
        name="scored_sums",
    )(me, mine, theirs)


def finish_kernel(
    me_ref, positions_ref, gain_ref, x_ref, later_ref, sums_ref, row_grads_ref, between_ref, within_ref
):
    own = x_ref.shape[0]
    x = x_ref[...].astype(F32)
    hidden = x + sums_ref[:own]
    picks = row_picks(positions_ref[...] - me_ref[0] * own, own)
    last = dot_tn(picks, row_grads_ref[...].astype(BF16))
    cotangent = jnp.where(me_ref[2] == 1, last, later_ref[...].astype(F32))
    inv_x = inv_rms(x)
    scaled = sums_ref[own:] * gain_ref[...].astype(F32)
    mean = jnp.mean(scaled * x, axis=-1, keepdims=True)
    returned = cotangent + inv_x * scaled - x * (inv_x * inv_x * inv_x * mean)
    odd = me_ref[1] == 1
    between_ref[...] = jnp.where(odd, hidden, returned).astype(BF16)
    within_ref[...] = jnp.where(odd, returned, hidden).astype(BF16)


def finish_part(me, positions, gain, x_own, later_own, sums, row_grads):
    vmem = pl.BlockSpec(memory_space=pltpu.VMEM)
    smem = pl.BlockSpec(memory_space=pltpu.SMEM)
    return pl.pallas_call(
        finish_kernel,
        out_shape=[jax.ShapeDtypeStruct(x_own.shape, BF16)] * 2,
        in_specs=[smem] + [vmem] * 6,
        out_specs=[vmem] * 2,
        compiler_params=pltpu.CompilerParams(vmem_limit_bytes=VMEM_LIMIT),
        name="finish",
    )(me, positions, gain, x_own, later_own, sums, row_grads)


def rank_grad(reward_scores, rankings):
    slots = jnp.arange(RESP)
    order_hot = (rankings[0][:, None] == slots[None, :]).astype(F32)
    ordered = jnp.sum(order_hot * reward_scores[None, :], axis=1)
    exp_order = jnp.exp(ordered)
    upper = (slots[:, None] >= slots[None, :]).astype(F32)
    suffix = jnp.sum(exp_order[:, None] * upper, axis=0)
    cumulative = jnp.sum((1.0 / suffix)[None, :] * upper, axis=1)
    grad_order = LOSS_SCALE * (exp_order * cumulative - 1.0)
    return jnp.sum(order_hot * grad_order[:, None], axis=0)


def gather_ring(block):
    count = lax.axis_size("tensor")
    blocks, offsets = [block], [0]
    up = down = block
    for step in range(1, count // 2 + 1):
        up = shift(up, 1)
        blocks.append(up)
        offsets.append(-step)
        if step < count - count // 2:
            down = shift(down, -1)
            blocks.append(down)
            offsets.append(step)
    return blocks, offsets


def scatter_ring(weights, far_mixed, far_back, next_rows, rest_rows, back_offsets, sections):
    far = lax.axis_size("tensor") // 2
    own = far_mixed.shape[0]
    none = jnp.zeros(far_mixed.shape, F32)
    up, down = shift(far_mixed, 1, sections), shift(far_back, -1, sections)
    terms = dict(zip(back_offsets[1:3], terms_of(weights, next_rows, own)))
    up = jnp.concatenate([up.astype(F32), none])
    down = jnp.concatenate([none, down.astype(F32)])
    for left in range(far - 1, 0, -1):
        up = (up.astype(F32) + terms[left].astype(F32)).astype(BF16)
        down = (down.astype(F32) + terms[-left].astype(F32)).astype(BF16)
        if left == far - 1:
            up, rest_rows = lax.optimization_barrier((up, rest_rows))
            terms.update(zip(back_offsets[3:], terms_of(weights, rest_rows, own)))
        up, down = shift(up, 1, sections), shift(down, -1, sections)
    return terms[0].astype(F32) + up.astype(F32) + down.astype(F32)


def sum_rows(value, sections):
    step = 1
    while step < lax.axis_size("tensor"):
        value = value + shift(value, step, sections)
        step *= 2
    return value


def shards(
    section_inputs,
    later_grad,
    attn_gain,
    w_query,
    w_key,
    w_value,
    w_out,
    final_gain,
    reward_head,
    rankings,
    lengths,
):
    x_own = section_inputs[0, 0]
    later_own = later_grad[0, 0]
    own_count = x_own.shape[0]
    tensor_count = lax.axis_size("tensor")
    tensor_pos = lax.axis_index("tensor")
    total_rows = own_count * tensor_count
    length = total_rows // RESP
    weights = (w_query[0], w_key[0], w_value[0], w_out[0])
    at_end = lax.axis_index("section") == lax.axis_size("section") - 1
    positions = jnp.arange(RESP) * length + lengths[0] - 1
    places = positions[:, None].astype(jnp.int32)
    odd = lax.axis_index("section") % 2
    me = jnp.stack([tensor_pos, odd, at_end]).astype(jnp.int32)

    last = lax.axis_size("section") - 1
    blocks, offsets = gather_ring(jnp.concatenate([x_own, later_own]))
    far = tensor_count // 2
    back_offsets = [far, far - 1, 1 - far, *range(2 - far, far - 1)]
    early = early_part(attn_gain, weights, blocks[:-1])

    def inner_section(early, late):
        parts = layer_part(me, attn_gain, weights, early, late, offsets, back_offsets, length)
        sums = scatter_ring(weights, *parts, back_offsets, range(last))
        return sums, jnp.zeros((RESP, x_own.shape[1]), F32)

    def last_section(early, late):
        qkv, rows_part = rows_part_of(
            me, places, attn_gain, weights, early, x_own, late, offsets, length
        )
        rows_hidden = sum_rows(rows_part, [last]).astype(BF16).astype(F32)
        inv_norm = inv_rms(rows_hidden)
        head_vec = final_gain.astype(F32) * reward_head.astype(F32)
        reward_scores = jnp.sum(rows_hidden * inv_norm * head_vec, axis=-1)
        scaled = rank_grad(reward_scores, rankings)[:, None] * head_vec
        row_grads = inv_norm * scaled - rows_hidden * inv_norm**3 * jnp.mean(
            scaled * rows_hidden, axis=-1, keepdims=True
        )
        row_grads = row_grads.astype(BF16).astype(F32)
        back_own = scored_part(
            me, places, row_grads, qkv, weights, tensor_count, length, last
        )
        return jnp.concatenate([jnp.zeros_like(back_own), back_own]), row_grads

    sums, row_grads = lax.cond(at_end, last_section, inner_section, early, blocks[-1])
    between, within = finish_part(me, places, attn_gain, x_own, later_own, sums, row_grads)
    between, within = swap_sections(between, 1), swap_sections(within, 0)
    even = lax.axis_index("section") % 2 == 0
    arrived = jnp.where(even, between, within)
    sent_back = jnp.where(even, within, between)
    return (arrived[None, None], sent_back[None, None])


def solution(mesh):
    return jax.shard_map(
        shards,
        mesh=mesh,
        in_specs=(
            P("section", None, "tensor", None),
            P("section", None, "tensor", None),
            P("section", None),
            P("section", None, "tensor"),
            P("section", None, "tensor"),
            P("section", None, "tensor"),
            P("section", "tensor", None),
            P(),
            P(),
            P(),
            P(),
        ),
        out_specs=(P("section", None, "tensor", None), P("section", None, "tensor", None)),
        check_vma=False,
    )
```
